256 devices in a mesh: dp: 2 (over z_hi), mode: 16 (over x, z_lo), tm: 8 (over y, core).
Axes of the slice: x: 4, y: 4, z: 8 (z_hi: 2, z_lo: 4; z = z_hi * 4 + z_lo), core: 2. Of those that a mesh axis runs over, the one named last changes fastest.
Arguments:
- input_field: float32 [2, 16, 32, 16384], P(None, 'dp', 'mode', 'tm'), parts along dimension 1, may hold values from -6 to 6
- target_field: float32 [2, 16, 32, 16384], P(None, 'dp', 'mode', 'tm'), parts along dimension 1, may hold values from -6 to 6
- margin: float32 [32, 32, 16], P('mode'), may hold values from -0.25 to 0.25
- pair_index: int32 [16, 2], replicated, may hold values from 0 to 31
- mode_beta: float32 [1024, 32, 3], P(None, 'mode'), may hold values from -2 to 2
- segment_kind: int32 [1], replicated, may hold values from 0 to 1023
Outputs:
- field_gradient: float32 [2, 16, 32, 16384], P(None, 'dp', 'mode', 'tm'), parts along dimension 1
The draws below stay inside these ranges and needn't reach their ends.
There are 2 independent parts, one for each index of `dp`. The reference program is written for one: setup_inputs(seed, part) draws one part's arguments, and reference() takes and returns one part's arrays. A program takes and returns all parts, laid end to end along the dimension named above; an argument that names none is the same for every part. Nothing has to cross between parts.
All inputs are finite; a program needn't handle non-finite values.
Results may differ from the reference program's by a relative error of at most 0.00011.
Values sent between devices are 32-bit elements; how exact they have to be, the bound alone decides.
No kernel may reach another device: no remote copies, remote signals or barrier semaphores. Data moves between devices by JAX's collectives and lax.ppermute only.
A program may use at most 128 MiB of HBM per device.

```python
import jax
import jax.numpy as jnp
from jax import lax

PULSES = 8
NT = 16384
PAIRS = 16
STEPS = 1
KINDS = 1024
MODES = 32


def set_ends(array, own_key, low, largest):
    spot = [jax.random.randint(jax.random.fold_in(own_key, axis), (), 0, length) for axis, length in enumerate(array.shape)]
    widest = array.shape.index(max(array.shape))
    neighbour = spot[:widest] + [(spot[widest] + 1) % array.shape[widest]] + spot[widest + 1:]
    return array.at[tuple(spot)].set(low).at[tuple(neighbour)].set(largest)


def steps_of(rng, dims, split, low, high):
    factor_of, own = 1.0, jax.random.fold_in(rng, 6)
    for dim, blocks in split:
        heights = jnp.exp(jax.random.uniform(jax.random.fold_in(own, dim), (blocks,), jnp.float32, low / len(split), high / len(split)))
        factor_of = factor_of * jnp.repeat(heights, dims[dim] // blocks).reshape([-1 if axis == dim else 1 for axis in range(len(dims))])
    return factor_of


def normal_values(stream_key, shape, spread, most, shards=(), kind=jnp.bfloat16):
    drawn = jax.random.normal(stream_key, shape, jnp.float32) * spread
    if len(shards) > 0:
        drawn = steps_of(stream_key, shape, shards, -0.22, 0.18) * drawn
    return jnp.clip(drawn, min=-most, max=most).astype(kind)


def setup_inputs(seed: int = 0, part: int = 0) -> dict:
    key_list = jax.random.split(jax.random.key(seed), 7)
    own_keys = jax.random.split(jax.random.fold_in(key_list[6], part), 7)
    input_field = normal_values(own_keys[0], (2, PULSES, MODES, NT), 1.0, 6.0, ((2, 16), (3, 8)), jnp.float32)
    target_field = normal_values(own_keys[1], (2, PULSES, MODES, NT), 1.0, 6.0, ((2, 16), (3, 8)), jnp.float32)
    margin = normal_values(key_list[2], (MODES, MODES, PAIRS), (MODES * PAIRS) ** -0.5, 0.25, ((0, 16),), jnp.float32)
    pair_index = set_ends(jax.random.randint(key_list[3], (PAIRS, 2), 0, MODES), jax.random.fold_in(key_list[3], 1), 0, MODES - 1).astype(jnp.int32)
    mode_beta = jnp.clip(jax.random.uniform(key_list[4], (KINDS, MODES, 3), jnp.float32, -2.0, 2.0) * steps_of(key_list[4], (KINDS, MODES, 3), ((1, 16),), -0.4, 0.0), -2.0, 2.0)
    segment_kind = jax.random.randint(key_list[5], (STEPS,), 0, KINDS).astype(jnp.int32)
    return dict(input_field=input_field, target_field=target_field, margin=margin, pair_index=pair_index, mode_beta=mode_beta, segment_kind=segment_kind)


kerr_scale = 0.1

def phases(mode_table):
    index = jnp.arange(NT, dtype=jnp.int32)
    signed = jnp.where(index < NT // 2, index, index - NT).astype(jnp.float32)
    omega = signed * (8.0 / NT)
    return mode_table[:, 0:1] * omega + mode_table[:, 1:2] * omega ** 2 / 2.0 + mode_table[:, 2:3] * omega ** 3 / 6.0

def disperse(pulse_field, phase):
    values = pulse_field[0] + 1j * pulse_field[1]
    spectrum = jnp.fft.fft(values, axis=-1) * jnp.exp(1j * phase)[None]
    result = jnp.fft.ifft(spectrum, axis=-1)
    return jnp.stack([jnp.real(result), jnp.imag(result)])

def nonlinear(pulse_field, margin, pair_index):

    def single(pulse):
        left = pulse[:, pair_index[:, 0], :]
        right = pulse[:, pair_index[:, 1], :]
        prod_real = left[0] * right[0] - left[1] * right[1]
        prod_imag = left[0] * right[1] + left[1] * right[0]
        coup_real = jnp.einsum('pnj,js->pns', margin, prod_real, precision=lax.Precision.HIGHEST)
        coup_imag = jnp.einsum('pnj,js->pns', margin, prod_imag, precision=lax.Precision.HIGHEST)
        non_real = lax.optimization_barrier(jnp.sum(coup_real * pulse[0][None] + coup_imag * pulse[1][None], axis=1))
        non_imag = lax.optimization_barrier(jnp.sum(coup_imag * pulse[0][None] - coup_real * pulse[1][None], axis=1))
        return jnp.stack([-kerr_scale * non_imag, kerr_scale * non_real])
    mapped = lax.map(single, jnp.moveaxis(pulse_field, 1, 0))
    return jnp.moveaxis(mapped, 0, 1)

def forward(pulse_field, margin, pair_index, mode_beta, segment_kind):
    for segment in range(STEPS):
        phase = phases(mode_beta[segment_kind[segment]])
        pulse_field = disperse(pulse_field, phase)
        pulse_field = pulse_field + nonlinear(pulse_field, margin, pair_index)
    return pulse_field

def reference(input_field, target_field, margin, pair_index, mode_beta, segment_kind):

    def misfit(pulse_field):
        output_field = forward(pulse_field, margin, pair_index, mode_beta, segment_kind)
        return jnp.sum((output_field - target_field) ** 2)
    value, pullback = jax.vjp(misfit, input_field)
    gradient = pullback(jnp.ones_like(value))[0]
    return gradient
```

```python
import jax
import jax.numpy as jnp
import numpy as np
from jax import lax
from jax.experimental import pallas as pl
from jax.experimental.pallas import tpu as pltpu
from jax.sharding import PartitionSpec as P

f32, bf16 = jnp.float32, jnp.bfloat16
kerr_scale = 0.1
SIDE = 128
TOTAL = SIDE * SIDE
MODES, PAIRS = 32, 16
OWNERS = 16
TIMES = 8
BLOCK = 72


def dft_parts():
    a = np.arange(SIDE)
    angle = 2.0 * np.pi * (np.outer(a, a) % SIDE) / SIDE
    parts = []
    for table in (np.cos(angle), np.sin(angle)):
        head = table.astype(np.float32).astype(bf16)
        parts += [head, (table - head.astype(np.float64)).astype(np.float32).astype(bf16)]
    return np.stack(parts)


def twist_parts():
    a = np.arange(SIDE)
    angle = 2.0 * np.pi * np.outer(a, a) / TOTAL
    return np.stack([np.cos(angle), np.sin(angle)]).astype(np.float32)


def heads(x):
    head = x.astype(bf16)
    return head, (x - head.astype(f32)).astype(bf16)


def dot(a, b):
    return jnp.dot(a, b, preferred_element_type=f32)


def real_form(cos, sin):
    return jnp.concatenate(
        [jnp.concatenate([cos, sin], 1), jnp.concatenate([-sin, cos], 1)], 0
    )


def disperse_modes(series, dft, twist, phase, sign):
    ch, cl, sh, sl = (dft[q] for q in range(4))
    plus = (real_form(ch, sh), real_form(cl, sl))
    minus = (real_form(ch, -sh), real_form(cl, -sl))

    def left(form, x):
        head, rest = heads(x)
        return dot(
            jnp.concatenate([form[0], form[0], form[1]], 1),
            jnp.concatenate([head, rest, head], 0),
        )

    def right(form, x):
        head, rest = heads(x)
        return dot(
            jnp.concatenate([head, rest, head], 1),
            jnp.concatenate([form[0], form[0], form[1]], 0),
        )

    tc, ts = twist[0], twist[1]
    result = []
    for m, (re, im) in enumerate(series):
        pc, ps = phase[0, m], sign * phase[1, m]
        y = left(plus, jnp.concatenate([re, im], 0))
        yr, yi = y[:SIDE], y[SIDE:]
        y = jnp.concatenate([yr * tc + yi * ts, yi * tc - yr * ts], 1)
        z = right(minus, y)
        zr, zi = z[:, :SIDE], z[:, SIDE:]
        z = jnp.concatenate([zr * pc - zi * ps, zr * ps + zi * pc], 1)
        y = right(plus, z)
        yr, yi = y[:, :SIDE], y[:, SIDE:]
        y = jnp.concatenate([yr * tc - yi * ts, yr * ts + yi * tc], 0)
        x = left(minus, y)
        result.append((x[:SIDE], x[SIDE:]))
    return result


def forward_kernel(rows_ref, margin_ref, dft_ref, twist_ref, phase_ref, out_ref):
    def series(what, m, part):
        return [
            rows_ref[pl.ds(s * 128 + what * 64 + part * 32 + m, 16, stride=2), :]
            for s in range(TIMES)
        ]

    fields = [
        tuple(jnp.concatenate(series(0, m, part), 0) for part in range(2)) for m in range(2)
    ]
    for m in range(2):
        for part in range(2):
            for s, chunk in enumerate(series(1, m, part)):
                for h in range(2):
                    spot = (2 * s + h) * BLOCK + 32 + m * 16 + part * 8
                    out_ref[spot : spot + 8, :] = chunk[8 * h : 8 * h + 8]
    margin = margin_ref[...]
    for k in range(OWNERS):
        out_ref[k * BLOCK + 64 : k * BLOCK + 72, :] = margin
    result = disperse_modes(fields, dft_ref, twist_ref, phase_ref, 1.0)
    for m in range(2):
        for part in range(2):
            for k in range(OWNERS):
                spot = k * BLOCK + m * 16 + part * 8
                out_ref[spot : spot + 8, :] = result[m][part][8 * k : 8 * k + 8]


def backward_kernel(rows_ref, dft_ref, twist_ref, phase_ref, out_ref):
    fields = [
        tuple(
            jnp.concatenate(
                [
                    rows_ref[k * 32 + m * 16 + part * 8 : k * 32 + m * 16 + part * 8 + 8, :]
                    for k in range(OWNERS)
                ],
                0,
            )
            for part in range(2)
        )
        for m in range(2)
    ]
    result = disperse_modes(fields, dft_ref, twist_ref, phase_ref, -1.0)
    for m in range(2):
        for part in range(2):
            for s in range(TIMES):
                out_ref[pl.ds(s * 64 + part * 32 + m, 16, stride=2), :] = result[m][part][
                    16 * s : 16 * s + 16
                ]


def kerr_kernel(pair_ref, rows_ref, out_ref, w_ref, gw_ref):
    def by_owner(row):
        return rows_ref[pl.ds(row, OWNERS, stride=BLOCK), :]

    def modes_at(first, part, s):
        return jnp.concatenate(
            [by_owner(first + m * 16 + part * 8 + s) for m in range(2)], 0
        )

    def own_mode(mode, block):
        spot = (mode >> 1) * block + (mode & 1) * 16
        return pl.ds(pl.multiple_of(spot, 8), 16)

    lane = lax.broadcasted_iota(jnp.int32, (128, 128), 1)

    def stacked(x):
        head = x.astype(bf16).astype(f32)
        return jnp.where(lane < 64, head, x - head).astype(bf16)

    quarters = [
        jnp.concatenate([by_owner(64 + m * 4 + q) for m in range(2)], 0) for q in range(4)
    ]
    whole = jnp.concatenate(quarters, 0)
    first_form = []
    for jr in range(4):
        mine = jnp.where(lane // 32 == jr, whole, 0.0)
        mine = mine + pltpu.roll(mine, 64, 1)
        mine = mine + pltpu.roll(mine, 32, 1)
        first_form.append(stacked(mine))
    first_form = jnp.concatenate(first_form, 0)
    second_form = jnp.concatenate(
        [stacked(jnp.concatenate([q] * 4, 0).T) for q in quarters], 0
    )

    for j in range(PAIRS):
        left = rows_ref[own_mode(pair_ref[j, 0], BLOCK), :]
        right = rows_ref[own_mode(pair_ref[j, 1], BLOCK), :]
        lr, li, rr, ri = left[:8], left[8:], right[:8], right[8:]
        w_ref[j * 16 : j * 16 + 8, :] = lr * rr - li * ri
        w_ref[j * 16 + 8 : j * 16 + 16, :] = lr * ri + li * rr

    def operand(re, im):
        head, rest = heads(jnp.concatenate([re, im], 1))
        return jnp.concatenate([head, rest, head, rest], 0)

    for s in range(8):
        ur, ui = modes_at(0, 0, s), modes_at(0, 1, s)
        coupled = dot(first_form, operand(ur, ui))
        total_re = total_im = 0.0
        for j in range(PAIRS):
            row = ((j % 4) * 4 + j // 4) * 32
            cr, ci = coupled[row : row + 32, :128], coupled[row : row + 32, 128:]
            wr = w_ref[j * 16 + s : j * 16 + s + 1, :]
            wi = w_ref[j * 16 + 8 + s : j * 16 + 9 + s, :]
            total_re += cr * wr + ci * wi
            total_im += cr * wi - ci * wr
        gr = 2.0 * (ur - kerr_scale * total_im - modes_at(32, 0, s))
        gi = 2.0 * (ui + kerr_scale * total_re - modes_at(32, 1, s))
        spread = dot(second_form, operand(kerr_scale * gi, -kerr_scale * gr))
        for j in range(PAIRS):
            sr, si = spread[j * 32 : j * 32 + 32, :128], spread[j * 32 : j * 32 + 32, 128:]
            wr = w_ref[j * 16 + s : j * 16 + s + 1, :]
            wi = w_ref[j * 16 + 8 + s : j * 16 + 9 + s, :]
            gr += sr * wr + si * wi
            gi += sr * wi - si * wr
            gw_ref[j * 16 + s : j * 16 + s + 1, :] = jnp.sum(
                sr * ur - si * ui, axis=0, keepdims=True
            )
            gw_ref[j * 16 + 8 + s : j * 16 + 9 + s, :] = jnp.sum(
                sr * ui + si * ur, axis=0, keepdims=True
            )
        for m in range(2):
            for part, g in enumerate((gr, gi)):
                out_ref[pl.ds(m * 16 + part * 8 + s, OWNERS, stride=32), :] = g[
                    m * 16 : m * 16 + 16
                ]

    for j in range(PAIRS):
        gwr, gwi = gw_ref[j * 16 : j * 16 + 8, :], gw_ref[j * 16 + 8 : j * 16 + 16, :]
        for here, other in ((0, 1), (1, 0)):
            factor = rows_ref[own_mode(pair_ref[j, other], BLOCK), :]
            fr, fi = factor[:8], factor[8:]
            spot = own_mode(pair_ref[j, here], 32)
            out_ref[spot, :] = out_ref[spot, :] + jnp.concatenate(
                [gwr * fr + gwi * fi, gwi * fr - gwr * fi], 0
            )


def call(kernel, rows, *args, scratch=(), specs=None):
    vmem = pl.BlockSpec(memory_space=pltpu.VMEM)
    return pl.pallas_call(
        kernel,
        out_shape=jax.ShapeDtypeStruct((rows, 128), f32),
        in_specs=specs or [vmem] * len(args),
        out_specs=vmem,
        scratch_shapes=list(scratch),
        compiler_params=pltpu.CompilerParams(vmem_limit_bytes=24 * 1024 * 1024),
    )(*args)


def phase_tables(mode_beta, segment_kind):
    table = lax.dynamic_slice_in_dim(mode_beta, segment_kind[0], 1, 0)[0]
    low = lax.broadcasted_iota(jnp.int32, (SIDE, SIDE), 0)
    high = lax.broadcasted_iota(jnp.int32, (SIDE, SIDE), 1)
    index = low + SIDE * high
    signed = jnp.where(index < TOTAL // 2, index, index - TOTAL).astype(f32)
    omega = signed * (8.0 / TOTAL)
    phase = (
        table[:, 0, None, None] * omega
        + table[:, 1, None, None] * omega**2 / 2.0
        + table[:, 2, None, None] * omega**3 / 6.0
    )
    return jnp.stack([jnp.cos(phase), jnp.sin(phase)]) * (1.0 / TOTAL)


def by_pulse(field):
    return field.reshape(2, 8, 2, 16, 128).transpose(1, 0, 3, 2, 4).reshape(8, 64, 128)


def on_device(input_field, target_field, margin, pair_index, mode_beta, segment_kind):
    dft, twist = jnp.asarray(dft_parts()), jnp.asarray(twist_parts())
    phase = phase_tables(mode_beta, segment_kind)
    coupling = margin.reshape(2, 16, 2, 16).transpose(0, 3, 2, 1).reshape(8, 128)
    both = jnp.concatenate([by_pulse(input_field), by_pulse(target_field)], 1)
    both = lax.all_to_all(both, "tm", 0, 0, tiled=True).reshape(1024, 128)
    packed = call(forward_kernel, OWNERS * BLOCK, both, coupling, dft, twist, phase)
    packed = lax.all_to_all(packed.reshape(OWNERS, BLOCK, 128), "mode", 0, 0, tiled=True)
    vmem = pl.BlockSpec(memory_space=pltpu.VMEM)
    cotangent = call(
        kerr_kernel,
        512,
        pair_index,
        packed.reshape(OWNERS * BLOCK, 128),
        scratch=[pltpu.VMEM((256, 128), f32)] * 2,
        specs=[pl.BlockSpec(memory_space=pltpu.SMEM), vmem],
    )
    cotangent = lax.all_to_all(cotangent.reshape(OWNERS, 32, 128), "mode", 0, 0, tiled=True)
    gradient = call(backward_kernel, 512, cotangent.reshape(512, 128), dft, twist, phase)
    gradient = lax.all_to_all(gradient.reshape(8, 64, 128), "tm", 0, 0, tiled=True)
    gradient = gradient.reshape(8, 2, 16, 2, 128).transpose(1, 0, 3, 2, 4)
    return gradient.reshape(2, 8, 2, 2048)


def solution(mesh):
    field = P(None, "dp", "mode", "tm")
    return jax.shard_map(
        on_device,
        mesh=mesh,
        in_specs=(field, field, P("mode", None, None), P(), P(None, "mode", None), P()),
        out_specs=field,
        check_vma=False,
    )
```

```python
import jax
import jax.numpy as jnp
import numpy as np
from jax import lax
from jax.experimental import pallas as pl
from jax.experimental.pallas import tpu as pltpu
from jax.sharding import PartitionSpec as P

f32, bf16 = jnp.float32, jnp.bfloat16
kerr_scale = 0.1
SIDE = 128
TOTAL = SIDE * SIDE
MODES, PAIRS = 32, 16
OWNERS = 16
TIMES = 8
BLOCK = 72


def dft_parts():
    a = np.arange(SIDE)
    angle = 2.0 * np.pi * (np.outer(a, a) % SIDE) / SIDE
    parts = []
    for table in (np.cos(angle), np.sin(angle)):
        head = table.astype(np.float32).astype(bf16)
        parts += [head, (table - head.astype(np.float64)).astype(np.float32).astype(bf16)]
    return np.stack(parts)


def twist_parts():
    a = np.arange(SIDE)
    angle = 2.0 * np.pi * np.outer(a, a) / TOTAL
    return np.stack([np.cos(angle), np.sin(angle)]).astype(np.float32)


def heads(x):
    head = x.astype(bf16)
    return head, (x - head.astype(f32)).astype(bf16)


def dot(a, b):
    return jnp.dot(a, b, preferred_element_type=f32)


def real_form(cos, sin):
    return jnp.concatenate(
        [jnp.concatenate([cos, sin], 1), jnp.concatenate([-sin, cos], 1)], 0
    )


def disperse_modes(series, dft, twist, phase, sign):
    ch, cl, sh, sl = (dft[q] for q in range(4))
    plus = (real_form(ch, sh), real_form(cl, sl))
    minus = (real_form(ch, -sh), real_form(cl, -sl))

    def left(form, x):
        head, rest = heads(x)
        return dot(
            jnp.concatenate([form[0], form[0], form[1]], 1),
            jnp.concatenate([head, rest, head], 0),
        )

    def right(form, x):
        head, rest = heads(x)
        return dot(
            jnp.concatenate([head, rest, head], 1),
            jnp.concatenate([form[0], form[0], form[1]], 0),
        )

    tc, ts = twist[0], twist[1]
    result = []
    for m, (re, im) in enumerate(series):
        pc, ps = phase[0, m], sign * phase[1, m]
        y = left(plus, jnp.concatenate([re, im], 0))
        yr, yi = y[:SIDE], y[SIDE:]
        y = jnp.concatenate([yr * tc + yi * ts, yi * tc - yr * ts], 1)
        z = right(minus, y)
        zr, zi = z[:, :SIDE], z[:, SIDE:]
        z = jnp.concatenate([zr * pc - zi * ps, zr * ps + zi * pc], 1)
        y = right(plus, z)
        yr, yi = y[:, :SIDE], y[:, SIDE:]
        y = jnp.concatenate([yr * tc - yi * ts, yr * ts + yi * tc], 0)
        x = left(minus, y)
        result.append((x[:SIDE], x[SIDE:]))
    return result


def gather_kernel(
    kind_ref, beta_hbm, margin_hbm, field_ref, target_ref,
    out_ref, phase_ref, coupling_ref,
    beta_ref, margin_ref, held_ref, small_sems, sems,
):
    small = [
        pltpu.make_async_copy(there, here, small_sems.at[q])
        for q, (there, here) in enumerate(
            ((beta_hbm, beta_ref), (margin_hbm, margin_ref))
        )
    ]
    for copy in small:
        copy.start()
    order = [(b, what) for b in range(8) for what in range(2)]
    copies = {}
    for b, what in order:
        copies[b, what] = pltpu.make_async_copy(
            (field_ref, target_ref)[what].at[:, b], held_ref.at[what, b], sems.at[what, b]
        )
        copies[b, what].start()
    for copy in small:
        copy.wait()

    lane = lax.broadcasted_iota(jnp.int32, (128, 128), 1)
    source = lax.broadcasted_iota(jnp.int32, (128, 128), 0)
    place = source // 32 * 32 + source % 2 * 16 + source % 32 // 2
    wide = jnp.zeros((16, 96), f32)
    flat = []
    for p in range(2):
        rows = jnp.concatenate([margin_ref[p], wide], 1)
        flat.append(
            sum(
                pltpu.roll(
                    jnp.concatenate([rows[4 * q + jr : 4 * q + jr + 1] for q in range(4)], 0),
                    32 * jr,
                    1,
                )
                if jr
                else jnp.concatenate([rows[4 * q : 4 * q + 1] for q in range(4)], 0)
                for jr in range(4)
            )
        )
    coupling_ref[...] = jnp.dot(
        jnp.concatenate(flat, 0),
        (place == lane).astype(f32),
        precision=lax.Precision.HIGHEST,
        preferred_element_type=f32,
    )

    kinds = lax.broadcasted_iota(jnp.int32, beta_ref.shape, 2)
    table = jnp.sum(jnp.where(kinds == kind_ref[0], beta_ref[...], 0.0), axis=2, keepdims=True)
    index = source + SIDE * lane
    signed = jnp.where(index < TOTAL // 2, index, index - TOTAL).astype(f32)
    omega = signed * (8.0 / TOTAL)
    for m in range(2):
        first, second, third = (table[q, m : m + 1] for q in range(3))
        phase = first * omega + second * omega**2 / 2.0 + third * omega**3 / 6.0
        phase_ref[0, m] = jnp.cos(phase) * (1.0 / TOTAL)
        phase_ref[1, m] = jnp.sin(phase) * (1.0 / TOTAL)

    for b, what in order:
        copies[b, what].wait()
        for part in range(2):
            spot = b * 128 + what * 64 + part * 32
            for k in range(16):
                out_ref[pl.ds(spot + k, 2, stride=16), :] = held_ref[
                    what, b, part, :, k * 128 : k * 128 + 128
                ]


def scatter_kernel(rows_ref, out_ref, held_ref, sems):
    copies = []
    for b in range(8):
        for part in range(2):
            for k in range(16):
                held_ref[b, part, :, k * 128 : k * 128 + 128] = rows_ref[
                    pl.ds(b * 64 + part * 32 + k, 2, stride=16), :
                ]
        copies.append(pltpu.make_async_copy(held_ref.at[b], out_ref.at[:, b], sems.at[b]))
        copies[-1].start()
    for copy in copies:
        copy.wait()


def forward_kernel(rows_ref, margin_ref, dft_ref, twist_ref, phase_ref, out_ref):
    def chunk(s, what, m, part):
        spot = s * 128 + what * 64 + part * 32 + m * 16
        return rows_ref[spot : spot + 16, :]

    fields = [
        tuple(
            jnp.concatenate([chunk(s, 0, m, part) for s in range(TIMES)], 0) for part in range(2)
        )
        for m in range(2)
    ]
    for m in range(2):
        for part in range(2):
            for s in range(TIMES):
                rows = chunk(s, 1, m, part)
                for h in range(2):
                    spot = (2 * s + h) * BLOCK + 32 + m * 16 + part * 8
                    out_ref[spot : spot + 8, :] = rows[8 * h : 8 * h + 8]
    margin = margin_ref[...]
    for k in range(OWNERS):
        out_ref[k * BLOCK + 64 : k * BLOCK + 72, :] = margin
    result = disperse_modes(fields, dft_ref, twist_ref, phase_ref, 1.0)
    for m in range(2):
        for part in range(2):
            for k in range(OWNERS):
                spot = k * BLOCK + m * 16 + part * 8
                out_ref[spot : spot + 8, :] = result[m][part][8 * k : 8 * k + 8]


def backward_kernel(rows_ref, dft_ref, twist_ref, phase_ref, out_ref):
    fields = [
        tuple(
            jnp.concatenate(
                [
                    rows_ref[k * 32 + m * 16 + part * 8 : k * 32 + m * 16 + part * 8 + 8, :]
                    for k in range(OWNERS)
                ],
                0,
            )
            for part in range(2)
        )
        for m in range(2)
    ]
    result = disperse_modes(fields, dft_ref, twist_ref, phase_ref, -1.0)
    for m in range(2):
        for part in range(2):
            for s in range(TIMES):
                spot = s * 64 + part * 32 + m * 16
                out_ref[spot : spot + 16, :] = result[m][part][16 * s : 16 * s + 16]


def kerr_kernel(pair_hbm, rows_ref, out_ref, pair_ref, w_ref, gw_ref, sem):
    pairs_in = pltpu.make_async_copy(pair_hbm, pair_ref, sem)
    pairs_in.start()

    def by_owner(row):
        return rows_ref[pl.ds(row, OWNERS, stride=BLOCK), :]

    def modes_at(first, part, s):
        return jnp.concatenate(
            [by_owner(first + m * 16 + part * 8 + s) for m in range(2)], 0
        )

    def own_mode(mode, block):
        spot = (mode >> 1) * block + (mode & 1) * 16
        return pl.ds(pl.multiple_of(spot, 8), 16)

    lane = lax.broadcasted_iota(jnp.int32, (128, 128), 1)

    def stacked(x):
        head = x.astype(bf16).astype(f32)
        return jnp.where(lane < 64, head, x - head).astype(bf16)

    quarters = [
        jnp.concatenate([by_owner(64 + m * 4 + q) for m in range(2)], 0) for q in range(4)
    ]
    whole = jnp.concatenate(quarters, 0)
    first_form = []
    for jr in range(4):
        mine = jnp.where(lane // 32 == jr, whole, 0.0)
        mine = mine + pltpu.roll(mine, 64, 1)
        mine = mine + pltpu.roll(mine, 32, 1)
        first_form.append(stacked(mine))
    first_form = jnp.concatenate(first_form, 0)
    second_form = jnp.concatenate(
        [stacked(jnp.concatenate([q] * 4, 0).T) for q in quarters], 0
    )

    pairs_in.wait()
    for j in range(PAIRS):
        left = rows_ref[own_mode(pair_ref[0, j], BLOCK), :]
        right = rows_ref[own_mode(pair_ref[1, j], BLOCK), :]
        lr, li, rr, ri = left[:8], left[8:], right[:8], right[8:]
        w_ref[j * 16 : j * 16 + 8, :] = lr * rr - li * ri
        w_ref[j * 16 + 8 : j * 16 + 16, :] = lr * ri + li * rr

    def operand(re, im):
        head, rest = heads(jnp.concatenate([re, im], 1))
        return jnp.concatenate([head, rest, head, rest], 0)

    for s in range(8):
        ur, ui = modes_at(0, 0, s), modes_at(0, 1, s)
        coupled = dot(first_form, operand(ur, ui))
        total_re = total_im = 0.0
        for j in range(PAIRS):
            row = ((j % 4) * 4 + j // 4) * 32
            cr, ci = coupled[row : row + 32, :128], coupled[row : row + 32, 128:]
            wr = w_ref[j * 16 + s : j * 16 + s + 1, :]
            wi = w_ref[j * 16 + 8 + s : j * 16 + 9 + s, :]
            total_re += cr * wr + ci * wi
            total_im += cr * wi - ci * wr
        gr = 2.0 * (ur - kerr_scale * total_im - modes_at(32, 0, s))
        gi = 2.0 * (ui + kerr_scale * total_re - modes_at(32, 1, s))
        spread = dot(second_form, operand(kerr_scale * gi, -kerr_scale * gr))
        for j in range(PAIRS):
            sr, si = spread[j * 32 : j * 32 + 32, :128], spread[j * 32 : j * 32 + 32, 128:]
            wr = w_ref[j * 16 + s : j * 16 + s + 1, :]
            wi = w_ref[j * 16 + 8 + s : j * 16 + 9 + s, :]
            gr += sr * wr + si * wi
            gi += sr * wi - si * wr
            gw_ref[j * 16 + s : j * 16 + s + 1, :] = jnp.sum(
                sr * ur - si * ui, axis=0, keepdims=True
            )
            gw_ref[j * 16 + 8 + s : j * 16 + 9 + s, :] = jnp.sum(
                sr * ui + si * ur, axis=0, keepdims=True
            )
        for m in range(2):
            for part, g in enumerate((gr, gi)):
                out_ref[pl.ds(m * 16 + part * 8 + s, OWNERS, stride=32), :] = g[
                    m * 16 : m * 16 + 16
                ]

    for j in range(PAIRS):
        gwr, gwi = gw_ref[j * 16 : j * 16 + 8, :], gw_ref[j * 16 + 8 : j * 16 + 16, :]
        for here, other in ((0, 1), (1, 0)):
            factor = rows_ref[own_mode(pair_ref[other, j], BLOCK), :]
            fr, fi = factor[:8], factor[8:]
            spot = own_mode(pair_ref[here, j], 32)
            out_ref[spot, :] = out_ref[spot, :] + jnp.concatenate(
                [gwr * fr + gwi * fi, gwi * fr - gwr * fi], 0
            )


VMEM, HBM = (pl.BlockSpec(memory_space=space) for space in (pltpu.VMEM, pltpu.HBM))


def in_hbm(x):
    return pltpu.with_memory_space_constraint(x, pltpu.HBM)


def call(kernel, shapes, *args, scratch=(), specs=None, out=pltpu.VMEM):
    shapes = [out(shape, f32) for shape in shapes]
    results = pl.pallas_call(
        kernel,
        out_shape=shapes,
        in_specs=specs or [VMEM] * len(args),
        out_specs=[pl.BlockSpec(memory_space=out)] * len(shapes),
        scratch_shapes=list(scratch),
        compiler_params=pltpu.CompilerParams(vmem_limit_bytes=24 * 1024 * 1024),
    )(*args)
    return results if len(shapes) > 1 else results[0]


def on_device(input_field, target_field, margin, pair_index, mode_beta, segment_kind):
    dft, twist = jnp.asarray(dft_parts()), jnp.asarray(twist_parts())
    both, phase, coupling = call(
        gather_kernel,
        [(1024, 128), (2, 2, SIDE, SIDE), (8, 128)],
        segment_kind,
        *map(
            in_hbm,
            (
                mode_beta.transpose(2, 1, 0),
                margin.transpose(0, 2, 1),
                input_field,
                target_field,
            ),
        ),
        scratch=[
            pltpu.VMEM((3, 2, mode_beta.shape[0]), f32),
            pltpu.VMEM((2, PAIRS, MODES), f32),
            pltpu.VMEM((2, 8, 2, 2, 2048), f32),
            pltpu.SemaphoreType.DMA((2,)),
            pltpu.SemaphoreType.DMA((2, 8)),
        ],
        specs=[pl.BlockSpec(memory_space=pltpu.SMEM)] + [HBM] * 4,
    )
    both = lax.all_to_all(both.reshape(8, 128, 128), "tm", 0, 0, tiled=True).reshape(1024, 128)
    packed = call(forward_kernel, [(OWNERS * BLOCK, 128)], both, coupling, dft, twist, phase)
    packed = lax.all_to_all(packed.reshape(OWNERS, BLOCK, 128), "mode", 0, 0, tiled=True)
    cotangent = call(
        kerr_kernel,
        [(512, 128)],
        in_hbm(pair_index.T),
        packed.reshape(OWNERS * BLOCK, 128),
        scratch=[
            pltpu.SMEM((2, PAIRS), jnp.int32),
            pltpu.VMEM((256, 128), f32),
            pltpu.VMEM((256, 128), f32),
            pltpu.SemaphoreType.DMA,
        ],
        specs=[HBM, VMEM],
    )
    cotangent = lax.all_to_all(cotangent.reshape(OWNERS, 32, 128), "mode", 0, 0, tiled=True)
    gradient = call(
        backward_kernel, [(512, 128)], cotangent.reshape(512, 128), dft, twist, phase
    )
    gradient = lax.all_to_all(gradient.reshape(8, 64, 128), "tm", 0, 0, tiled=True)
    return call(
        scatter_kernel,
        [(2, 8, 2, 2048)],
        gradient.reshape(512, 128),
        scratch=[pltpu.VMEM((8, 2, 2, 2048), f32), pltpu.SemaphoreType.DMA((8,))],
        out=pltpu.HBM,
    )


def solution(mesh):
    field = P(None, "dp", "mode", "tm")
    return jax.shard_map(
        on_device,
        mesh=mesh,
        in_specs=(field, field, P("mode", None, None), P(), P(None, "mode", None), P()),
        out_specs=field,
        check_vma=False,
    )
```

```python
import jax
import jax.numpy as jnp
import numpy as np
from jax import lax
from jax.experimental import pallas as pl
from jax.experimental.pallas import tpu as pltpu
from jax.sharding import PartitionSpec as P

f32, bf16 = jnp.float32, jnp.bfloat16
kerr_scale = 0.1
SIDE = 128
TOTAL = SIDE * SIDE
MODES, PAIRS = 32, 16
OWNERS = 16
TIMES = 8
BLOCK = 72


def dft_parts():
    a = np.arange(SIDE)
    angle = 2.0 * np.pi * (np.outer(a, a) % SIDE) / SIDE
    parts = []
    for table in (np.cos(angle), np.sin(angle)):
        head = table.astype(np.float32).astype(bf16)
        parts += [head, (table - head.astype(np.float64)).astype(np.float32).astype(bf16)]
    return np.stack(parts)


def twist_parts():
    a = np.arange(SIDE)
    angle = 2.0 * np.pi * np.outer(a, a) / TOTAL
    return np.stack([np.cos(angle), np.sin(angle)]).astype(np.float32)


def heads(x):
    head = x.astype(bf16)
    return head, (x - head.astype(f32)).astype(bf16)


def dot(a, b):
    return jnp.dot(a, b, preferred_element_type=f32)


def real_form(cos, sin):
    return jnp.concatenate(
        [jnp.concatenate([cos, sin], 1), jnp.concatenate([-sin, cos], 1)], 0
    )


def disperse_modes(series, dft, twist, phase, sign):
    ch, cl, sh, sl = (dft[q] for q in range(4))
    plus = (real_form(ch, sh), real_form(cl, sl))
    minus = (real_form(ch, -sh), real_form(cl, -sl))

    def left(form, x):
        head, rest = heads(x)
        return dot(
            jnp.concatenate([form[0], form[0], form[1]], 1),
            jnp.concatenate([head, rest, head], 0),
        )

    def right(form, x):
        head, rest = heads(x)
        return dot(
            jnp.concatenate([head, rest, head], 1),
            jnp.concatenate([form[0], form[0], form[1]], 0),
        )

    def beside(parts):
        return jnp.concatenate(parts, 1)

    def below(parts):
        return jnp.concatenate(parts, 0)

    def quadrants(x):
        return (x[:SIDE, :SIDE], x[SIDE:, :SIDE]), (x[:SIDE, SIDE:], x[SIDE:, SIDE:])

    tc, ts = twist[0], twist[1]
    y = quadrants(left(plus, beside([below(pair) for pair in series])))
    y = below([beside([yr * tc + yi * ts, yi * tc - yr * ts]) for yr, yi in y])
    z = right(minus, y)
    turned = []
    for m in range(2):
        zr, zi = z[m * SIDE : (m + 1) * SIDE, :SIDE], z[m * SIDE : (m + 1) * SIDE, SIDE:]
        pc, ps = phase[0, m], sign * phase[1, m]
        turned.append(beside([zr * pc - zi * ps, zr * ps + zi * pc]))
    y = right(plus, below(turned))
    twisted = []
    for m in range(2):
        yr, yi = y[m * SIDE : (m + 1) * SIDE, :SIDE], y[m * SIDE : (m + 1) * SIDE, SIDE:]
        twisted.append(below([yr * tc - yi * ts, yr * ts + yi * tc]))
    return quadrants(left(minus, beside(twisted)))


def cos_sin(angle):
    turn = jnp.floor(angle * (2.0 / np.pi) + 0.5)
    x = angle - turn * 1.5703125
    x = x - turn * 4.837512969970703e-4
    x = x - turn * 7.549789954891882e-8
    z = x * x
    sine = x + x * z * (-1.6666654611e-1 + z * (8.3321608736e-3 - z * 1.9515295891e-4))
    cosine = 1.0 - 0.5 * z + z * z * (
        4.166664568298827e-2 + z * (-1.388731625493765e-3 + z * 2.443315711809948e-5)
    )
    quarter = turn.astype(jnp.int32)
    odd = quarter & 1 == 1
    first, second = jnp.where(odd, sine, cosine), jnp.where(odd, cosine, sine)
    return (
        jnp.where((quarter + 1) & 2 == 2, -first, first),
        jnp.where(quarter & 2 == 2, -second, second),
    )


def gather_kernel(
    kind_ref, beta_hbm, margin_hbm, pair_hbm, field_ref, target_ref,
    out_ref, phase_ref, coupling_ref, pair_ref,
    beta_ref, margin_ref, held_ref, small_sems, sems,
):
    small = [
        pltpu.make_async_copy(there, here, small_sems.at[q])
        for q, (there, here) in enumerate(
            ((beta_hbm, beta_ref), (margin_hbm, margin_ref), (pair_hbm, pair_ref))
        )
    ]
    for copy in small:
        copy.start()
    order = [(b, what) for b in range(8) for what in range(2)]
    copies = {}
    for b, what in order:
        copies[b, what] = pltpu.make_async_copy(
            (field_ref, target_ref)[what].at[:, b], held_ref.at[what, b], sems.at[what, b]
        )
        copies[b, what].start()
    small[0].wait()
    small[1].wait()

    lane = lax.broadcasted_iota(jnp.int32, (128, 128), 1)
    source = lax.broadcasted_iota(jnp.int32, (128, 128), 0)
    place = source // 32 * 32 + source % 2 * 16 + source % 32 // 2
    wide = jnp.zeros((16, 96), f32)
    flat = []
    for p in range(2):
        rows = jnp.concatenate([margin_ref[p], wide], 1)
        flat.append(
            sum(
                pltpu.roll(
                    jnp.concatenate([rows[4 * q + jr : 4 * q + jr + 1] for q in range(4)], 0),
                    32 * jr,
                    1,
                )
                if jr
                else jnp.concatenate([rows[4 * q : 4 * q + 1] for q in range(4)], 0)
                for jr in range(4)
            )
        )
    coupling_ref[...] = jnp.dot(
        jnp.concatenate(flat, 0),
        (place == lane).astype(f32),
        precision=lax.Precision.HIGHEST,
        preferred_element_type=f32,
    )

    kinds = lax.broadcasted_iota(jnp.int32, beta_ref.shape, 2)
    table = jnp.sum(jnp.where(kinds == kind_ref[0], beta_ref[...], 0.0), axis=2, keepdims=True)
    index = source + SIDE * lane
    signed = jnp.where(index < TOTAL // 2, index, index - TOTAL).astype(f32)
    omega = signed * (8.0 / TOTAL)
    for m in range(2):
        first, second, third = (table[q, m : m + 1] for q in range(3))
        phase = first * omega + second * omega**2 / 2.0 + third * omega**3 / 6.0
        cosine, sine = cos_sin(phase)
        phase_ref[0, m] = cosine * (1.0 / TOTAL)
        phase_ref[1, m] = sine * (1.0 / TOTAL)

    for b, what in order:
        copies[b, what].wait()
        for part in range(2):
            spot = b * 128 + what * 64 + part * 32
            for k in range(16):
                out_ref[pl.ds(spot + k, 2, stride=16), :] = held_ref[
                    what, b, part, :, k * 128 : k * 128 + 128
                ]
    small[2].wait()


def scatter_kernel(rows_ref, out_ref, held_ref, sems):
    copies = []
    for b in range(8):
        for part in range(2):
            for k in range(16):
                held_ref[b, part, :, k * 128 : k * 128 + 128] = rows_ref[
                    pl.ds(b * 64 + part * 32 + k, 2, stride=16), :
                ]
        copies.append(pltpu.make_async_copy(held_ref.at[b], out_ref.at[:, b], sems.at[b]))
        copies[-1].start()
    for copy in copies:
        copy.wait()


def forward_kernel(rows_ref, margin_ref, dft_ref, twist_ref, phase_ref, out_ref):
    def chunk(s, what, m, part):
        spot = s * 128 + what * 64 + part * 32 + m * 16
        return rows_ref[spot : spot + 16, :]

    fields = [
        tuple(
            jnp.concatenate([chunk(s, 0, m, part) for s in range(TIMES)], 0) for part in range(2)
        )
        for m in range(2)
    ]
    for m in range(2):
        for part in range(2):
            for s in range(TIMES):
                rows = chunk(s, 1, m, part)
                for h in range(2):
                    spot = (2 * s + h) * BLOCK + 32 + m * 16 + part * 8
                    out_ref[spot : spot + 8, :] = rows[8 * h : 8 * h + 8]
    margin = margin_ref[...]
    for k in range(OWNERS):
        out_ref[k * BLOCK + 64 : k * BLOCK + 72, :] = margin
    result = disperse_modes(fields, dft_ref, twist_ref, phase_ref, 1.0)
    for m in range(2):
        for part in range(2):
            for k in range(OWNERS):
                spot = k * BLOCK + m * 16 + part * 8
                out_ref[spot : spot + 8, :] = result[m][part][8 * k : 8 * k + 8]


def backward_kernel(rows_ref, dft_ref, twist_ref, phase_ref, out_ref):
    fields = [
        tuple(
            jnp.concatenate(
                [
                    rows_ref[k * 32 + m * 16 + part * 8 : k * 32 + m * 16 + part * 8 + 8, :]
                    for k in range(OWNERS)
                ],
                0,
            )
            for part in range(2)
        )
        for m in range(2)
    ]
    result = disperse_modes(fields, dft_ref, twist_ref, phase_ref, -1.0)
    for m in range(2):
        for part in range(2):
            for s in range(TIMES):
                spot = s * 64 + part * 32 + m * 16
                out_ref[spot : spot + 16, :] = result[m][part][16 * s : 16 * s + 16]


def kerr_kernel(pair_vmem, rows_ref, out_ref, pair_ref, w_ref, gw_ref, other_ref, sem):
    pairs_in = pltpu.make_async_copy(pair_vmem, pair_ref, sem)
    pairs_in.start()

    def by_owner(row):
        return rows_ref[pl.ds(row, OWNERS, stride=BLOCK), :]

    def modes_at(first, part, s):
        return jnp.concatenate(
            [by_owner(first + m * 16 + part * 8 + s) for m in range(2)], 0
        )

    def own_mode(mode, block):
        spot = (mode >> 1) * block + (mode & 1) * 16
        return pl.ds(pl.multiple_of(spot, 8), 16)

    other_ref[...] = jnp.zeros_like(other_ref)
    lane = lax.broadcasted_iota(jnp.int32, (128, 128), 1)

    def stacked(x):
        head = x.astype(bf16).astype(f32)
        return jnp.where(lane < 64, head, x - head).astype(bf16)

    quarters = [
        jnp.concatenate([by_owner(64 + m * 4 + q) for m in range(2)], 0) for q in range(4)
    ]
    whole = jnp.concatenate(quarters, 0)
    first_form = []
    for jr in range(4):
        mine = jnp.where(lane // 32 == jr, whole, 0.0)
        mine = mine + pltpu.roll(mine, 64, 1)
        mine = mine + pltpu.roll(mine, 32, 1)
        first_form.append(stacked(mine))
    first_form = jnp.concatenate(first_form, 0)
    second_form = jnp.concatenate(
        [stacked(jnp.concatenate([q] * 4, 0).T) for q in quarters], 0
    )

    pairs_in.wait()
    for j in range(PAIRS):
        left = rows_ref[own_mode(pair_ref[0, j], BLOCK), :]
        right = rows_ref[own_mode(pair_ref[1, j], BLOCK), :]
        lr, li, rr, ri = left[:8], left[8:], right[:8], right[8:]
        w_ref[j * 16 : j * 16 + 8, :] = lr * rr - li * ri
        w_ref[j * 16 + 8 : j * 16 + 16, :] = lr * ri + li * rr

    def operand(re, im):
        head, rest = heads(jnp.concatenate([re, im], 1))
        return jnp.concatenate([head, rest, head, rest], 0)

    for s in range(8):
        ur, ui = modes_at(0, 0, s), modes_at(0, 1, s)
        coupled = dot(first_form, operand(ur, ui))
        total_re = total_im = 0.0
        for j in range(PAIRS):
            row = ((j % 4) * 4 + j // 4) * 32
            cr, ci = coupled[row : row + 32, :128], coupled[row : row + 32, 128:]
            wr = w_ref[j * 16 + s : j * 16 + s + 1, :]
            wi = w_ref[j * 16 + 8 + s : j * 16 + 9 + s, :]
            total_re += cr * wr + ci * wi
            total_im += cr * wi - ci * wr
        gr = 2.0 * (ur - kerr_scale * total_im - modes_at(32, 0, s))
        gi = 2.0 * (ui + kerr_scale * total_re - modes_at(32, 1, s))
        spread = dot(second_form, operand(kerr_scale * gi, -kerr_scale * gr))
        for j in range(PAIRS):
            sr, si = spread[j * 32 : j * 32 + 32, :128], spread[j * 32 : j * 32 + 32, 128:]
            wr = w_ref[j * 16 + s : j * 16 + s + 1, :]
            wi = w_ref[j * 16 + 8 + s : j * 16 + 9 + s, :]
            gr += sr * wr + si * wi
            gi += sr * wi - si * wr
            gw_ref[j * 16 + s : j * 16 + s + 1, :] = jnp.sum(
                sr * ur - si * ui, axis=0, keepdims=True
            )
            gw_ref[j * 16 + 8 + s : j * 16 + 9 + s, :] = jnp.sum(
                sr * ui + si * ur, axis=0, keepdims=True
            )
        for m in range(2):
            for part, g in enumerate((gr, gi)):
                out_ref[pl.ds(m * 16 + part * 8 + s, OWNERS, stride=32), :] = g[
                    m * 16 : m * 16 + 16
                ]

    for j in range(PAIRS):
        gwr, gwi = gw_ref[j * 16 : j * 16 + 8, :], gw_ref[j * 16 + 8 : j * 16 + 16, :]
        for here, other, sum_ref in ((0, 1, out_ref), (1, 0, other_ref)):
            factor = rows_ref[own_mode(pair_ref[other, j], BLOCK), :]
            fr, fi = factor[:8], factor[8:]
            spot = own_mode(pair_ref[here, j], 32)
            sum_ref[spot, :] = sum_ref[spot, :] + jnp.concatenate(
                [gwr * fr + gwi * fi, gwi * fr - gwr * fi], 0
            )
    out_ref[...] = out_ref[...] + other_ref[...]


VMEM, HBM = (pl.BlockSpec(memory_space=space) for space in (pltpu.VMEM, pltpu.HBM))


def in_hbm(x):
    return pltpu.with_memory_space_constraint(x, pltpu.HBM)


def call(kernel, shapes, *args, scratch=(), specs=None, out=pltpu.VMEM):
    shapes = [out(shape, f32) if type(shape) is tuple else shape for shape in shapes]
    results = pl.pallas_call(
        kernel,
        out_shape=shapes,
        in_specs=specs or [VMEM] * len(args),
        out_specs=[pl.BlockSpec(memory_space=out)] * len(shapes),
        scratch_shapes=list(scratch),
        compiler_params=pltpu.CompilerParams(vmem_limit_bytes=24 * 1024 * 1024),
    )(*args)
    return results if len(shapes) > 1 else results[0]


def on_device(input_field, target_field, margin, pair_index, mode_beta, segment_kind):
    dft, twist = jnp.asarray(dft_parts()), jnp.asarray(twist_parts())
    both, phase, coupling, pairs = call(
        gather_kernel,
        [(1024, 128), (2, 2, SIDE, SIDE), (8, 128), pltpu.VMEM((2, PAIRS), jnp.int32)],
        segment_kind,
        *map(
            in_hbm,
            (
                mode_beta.transpose(2, 1, 0),
                margin.transpose(0, 2, 1),
                pair_index.T,
                input_field,
                target_field,
            ),
        ),
        scratch=[
            pltpu.VMEM((3, 2, mode_beta.shape[0]), f32),
            pltpu.VMEM((2, PAIRS, MODES), f32),
            pltpu.VMEM((2, 8, 2, 2, 2048), f32),
            pltpu.SemaphoreType.DMA((3,)),
            pltpu.SemaphoreType.DMA((2, 8)),
        ],
        specs=[pl.BlockSpec(memory_space=pltpu.SMEM)] + [HBM] * 5,
    )
    both = lax.all_to_all(both.reshape(8, 128, 128), "tm", 0, 0, tiled=True).reshape(1024, 128)
    packed = call(forward_kernel, [(OWNERS * BLOCK, 128)], both, coupling, dft, twist, phase)
    packed = lax.all_to_all(packed.reshape(OWNERS, BLOCK, 128), "mode", 0, 0, tiled=True)
    cotangent = call(
        kerr_kernel,
        [(512, 128)],
        pairs,
        packed.reshape(OWNERS * BLOCK, 128),
        scratch=[
            pltpu.SMEM((2, PAIRS), jnp.int32),
            pltpu.VMEM((256, 128), f32),
            pltpu.VMEM((256, 128), f32),
            pltpu.VMEM((512, 128), f32),
            pltpu.SemaphoreType.DMA,
        ],
        specs=[VMEM, VMEM],
    )
    cotangent = lax.all_to_all(cotangent.reshape(OWNERS, 32, 128), "mode", 0, 0, tiled=True)
    gradient = call(
        backward_kernel, [(512, 128)], cotangent.reshape(512, 128), dft, twist, phase
    )
    gradient = lax.all_to_all(gradient.reshape(8, 64, 128), "tm", 0, 0, tiled=True)
    return call(
        scatter_kernel,
        [(2, 8, 2, 2048)],
        gradient.reshape(512, 128),
        scratch=[pltpu.VMEM((8, 2, 2, 2048), f32), pltpu.SemaphoreType.DMA((8,))],
        out=pltpu.HBM,
    )


def solution(mesh):
    field = P(None, "dp", "mode", "tm")
    return jax.shard_map(
        on_device,
        mesh=mesh,
        in_specs=(field, field, P("mode", None, None), P(), P(None, "mode", None), P()),
        out_specs=field,
        check_vma=False,
    )
```

```python
import jax
import jax.numpy as jnp
import numpy as np
from jax import lax
from jax.experimental import pallas as pl
from jax.experimental.pallas import tpu as pltpu
from jax.sharding import PartitionSpec as P

f32, bf16 = jnp.float32, jnp.bfloat16
kerr_scale = 0.1
SIDE = 128
TOTAL = SIDE * SIDE
MODES, PAIRS = 32, 16
OWNERS = 16
TIMES = 8
BLOCK = 72


def dft_parts():
    a = np.arange(SIDE)
    angle = 2.0 * np.pi * (np.outer(a, a) % SIDE) / SIDE
    parts = []
    for table in (np.cos(angle), np.sin(angle)):
        head = table.astype(np.float32).astype(bf16)
        parts += [head, (table - head.astype(np.float64)).astype(np.float32).astype(bf16)]
    return np.stack(parts)


def twist_parts():
    a = np.arange(SIDE)
    angle = 2.0 * np.pi * np.outer(a, a) / TOTAL
    return np.stack([np.cos(angle), np.sin(angle)]).astype(np.float32)


def heads(x):
    head = x.astype(bf16)
    return head, (x - head.astype(f32)).astype(bf16)


def dot(a, b):
    return jnp.dot(a, b, preferred_element_type=f32)


def real_form(cos, sin):
    return jnp.concatenate(
        [jnp.concatenate([cos, sin], 1), jnp.concatenate([-sin, cos], 1)], 0
    )


def disperse_modes(series, dft, twist, phase, sign):
    ch, cl, sh, sl = (dft[q] for q in range(4))
    plus = (real_form(ch, sh), real_form(cl, sl))
    minus = (real_form(ch, -sh), real_form(cl, -sl))

    def left(form, x):
        head, rest = heads(x)
        return dot(
            jnp.concatenate([form[0], form[0], form[1]], 1),
            jnp.concatenate([head, rest, head], 0),
        )

    def right(form, x):
        head, rest = heads(x)
        return dot(
            jnp.concatenate([head, rest, head], 1),
            jnp.concatenate([form[0], form[0], form[1]], 0),
        )

    def beside(parts):
        return jnp.concatenate(parts, 1)

    def below(parts):
        return jnp.concatenate(parts, 0)

    def quadrants(x):
        return (x[:SIDE, :SIDE], x[SIDE:, :SIDE]), (x[:SIDE, SIDE:], x[SIDE:, SIDE:])

    tc, ts = twist[0], twist[1]
    y = quadrants(left(plus, beside([below(pair) for pair in series])))
    y = below([beside([yr * tc + yi * ts, yi * tc - yr * ts]) for yr, yi in y])
    z = right(minus, y)
    turned = []
    for m in range(2):
        zr, zi = z[m * SIDE : (m + 1) * SIDE, :SIDE], z[m * SIDE : (m + 1) * SIDE, SIDE:]
        pc, ps = phase[0, m], sign * phase[1, m]
        turned.append(beside([zr * pc - zi * ps, zr * ps + zi * pc]))
    y = right(plus, below(turned))
    twisted = []
    for m in range(2):
        yr, yi = y[m * SIDE : (m + 1) * SIDE, :SIDE], y[m * SIDE : (m + 1) * SIDE, SIDE:]
        twisted.append(below([yr * tc - yi * ts, yr * ts + yi * tc]))
    return quadrants(left(minus, beside(twisted)))


def cos_sin(angle):
    turn = jnp.floor(angle * (2.0 / np.pi) + 0.5)
    x = angle - turn * 1.5703125
    x = x - turn * 4.837512969970703e-4
    x = x - turn * 7.549789954891882e-8
    z = x * x
    sine = x + x * z * (-1.6666654611e-1 + z * (8.3321608736e-3 - z * 1.9515295891e-4))
    cosine = 1.0 - 0.5 * z + z * z * (
        4.166664568298827e-2 + z * (-1.388731625493765e-3 + z * 2.443315711809948e-5)
    )
    quarter = turn.astype(jnp.int32)
    odd = quarter & 1 == 1
    first, second = jnp.where(odd, sine, cosine), jnp.where(odd, cosine, sine)
    return (
        jnp.where((quarter + 1) & 2 == 2, -first, first),
        jnp.where(quarter & 2 == 2, -second, second),
    )


def gather_kernel(
    kind_ref, beta_hbm, margin_hbm, pair_hbm, field_ref, target_ref,
    out_ref, phase_ref, coupling_ref, spot_ref,
    pair_ref, beta_ref, margin_ref, held_ref, small_sems, sems,
):
    small = [
        pltpu.make_async_copy(there, here, small_sems.at[q])
        for q, (there, here) in enumerate(
            ((beta_hbm, beta_ref), (margin_hbm, margin_ref), (pair_hbm, pair_ref))
        )
    ]
    for copy in small:
        copy.start()
    order = [(b, what) for b in range(8) for what in range(2)]
    copies = {}
    for b, what in order:
        copies[b, what] = pltpu.make_async_copy(
            (field_ref, target_ref)[what].at[:, b], held_ref.at[what, b], sems.at[what, b]
        )
        copies[b, what].start()

    for b, what in order:
        copies[b, what].wait()
        for part in range(2):
            spot = b * 128 + what * 64 + part * 32
            for k in range(16):
                out_ref[pl.ds(spot + k, 2, stride=16), :] = held_ref[
                    what, b, part, :, k * 128 : k * 128 + 128
                ]
    for copy in small:
        copy.wait()
    pair = pair_ref[...]
    for q, block in enumerate((BLOCK, 32)):
        spot_ref[2 * q : 2 * q + 2, :] = (pair >> 1) * block + (pair & 1) * 16
    lane = lax.broadcasted_iota(jnp.int32, (128, 128), 1)
    source = lax.broadcasted_iota(jnp.int32, (128, 128), 0)
    place = source // 32 * 32 + source % 2 * 16 + source % 32 // 2
    wide = jnp.zeros((16, 96), f32)
    flat = []
    for p in range(2):
        rows = jnp.concatenate([margin_ref[p], wide], 1)
        flat.append(
            sum(
                pltpu.roll(
                    jnp.concatenate([rows[4 * q + jr : 4 * q + jr + 1] for q in range(4)], 0),
                    32 * jr,
                    1,
                )
                if jr
                else jnp.concatenate([rows[4 * q : 4 * q + 1] for q in range(4)], 0)
                for jr in range(4)
            )
        )
    coupling_ref[...] = jnp.dot(
        jnp.concatenate(flat, 0),
        (place == lane).astype(f32),
        precision=lax.Precision.HIGHEST,
        preferred_element_type=f32,
    )

    kinds = lax.broadcasted_iota(jnp.int32, beta_ref.shape, 2)
    table = jnp.sum(jnp.where(kinds == kind_ref[0], beta_ref[...], 0.0), axis=2, keepdims=True)
    index = source + SIDE * lane
    signed = jnp.where(index < TOTAL // 2, index, index - TOTAL).astype(f32)
    omega = signed * (8.0 / TOTAL)
    for m in range(2):
        first, second, third = (table[q, m : m + 1] for q in range(3))
        phase = first * omega + second * omega**2 / 2.0 + third * omega**3 / 6.0
        cosine, sine = cos_sin(phase)
        phase_ref[0, m] = cosine * (1.0 / TOTAL)
        phase_ref[1, m] = sine * (1.0 / TOTAL)


def scatter_kernel(rows_ref, out_ref, held_ref, sems):
    copies = []
    for b in range(8):
        for part in range(2):
            for k in range(16):
                held_ref[b, part, :, k * 128 : k * 128 + 128] = rows_ref[
                    pl.ds(b * 64 + part * 32 + k, 2, stride=16), :
                ]
        copies.append(pltpu.make_async_copy(held_ref.at[b], out_ref.at[:, b], sems.at[b]))
        copies[-1].start()
    for copy in copies:
        copy.wait()


def forward_kernel(rows_ref, margin_ref, dft_ref, twist_ref, phase_ref, out_ref):
    def chunk(s, what, m, part):
        spot = s * 128 + what * 64 + part * 32 + m * 16
        return rows_ref[spot : spot + 16, :]

    fields = [
        tuple(
            jnp.concatenate([chunk(s, 0, m, part) for s in range(TIMES)], 0) for part in range(2)
        )
        for m in range(2)
    ]
    for m in range(2):
        for part in range(2):
            for s in range(TIMES):
                rows = chunk(s, 1, m, part)
                for h in range(2):
                    spot = (2 * s + h) * BLOCK + 32 + m * 16 + part * 8
                    out_ref[spot : spot + 8, :] = rows[8 * h : 8 * h + 8]
    margin = margin_ref[...]
    for k in range(OWNERS):
        out_ref[k * BLOCK + 64 : k * BLOCK + 72, :] = margin
    result = disperse_modes(fields, dft_ref, twist_ref, phase_ref, 1.0)
    for m in range(2):
        for part in range(2):
            for k in range(OWNERS):
                spot = k * BLOCK + m * 16 + part * 8
                out_ref[spot : spot + 8, :] = result[m][part][8 * k : 8 * k + 8]


def backward_kernel(rows_ref, dft_ref, twist_ref, phase_ref, out_ref):
    fields = [
        tuple(
            jnp.concatenate(
                [
                    rows_ref[k * 32 + m * 16 + part * 8 : k * 32 + m * 16 + part * 8 + 8, :]
                    for k in range(OWNERS)
                ],
                0,
            )
            for part in range(2)
        )
        for m in range(2)
    ]
    result = disperse_modes(fields, dft_ref, twist_ref, phase_ref, -1.0)
    for m in range(2):
        for part in range(2):
            for s in range(TIMES):
                spot = s * 64 + part * 32 + m * 16
                out_ref[spot : spot + 16, :] = result[m][part][16 * s : 16 * s + 16]


def kerr_kernel(spot_vmem, rows_ref, out_ref, spot_ref, w_ref, gw_ref, other_ref, sem):
    spots_in = pltpu.make_async_copy(spot_vmem, spot_ref, sem)
    spots_in.start()

    def by_owner(row):
        return rows_ref[pl.ds(row, OWNERS, stride=BLOCK), :]

    def modes_at(first, part, s):
        return jnp.concatenate(
            [by_owner(first + m * 16 + part * 8 + s) for m in range(2)], 0
        )

    def mode_rows(kind, j):
        return pl.ds(pl.multiple_of(spot_ref[kind, j], 8), 16)

    other_ref[...] = jnp.zeros_like(other_ref)
    lane = lax.broadcasted_iota(jnp.int32, (128, 128), 1)

    def stacked(x):
        head = x.astype(bf16).astype(f32)
        return jnp.where(lane < 64, head, x - head).astype(bf16)

    quarters = [
        jnp.concatenate([by_owner(64 + m * 4 + q) for m in range(2)], 0) for q in range(4)
    ]
    whole = jnp.concatenate(quarters, 0)
    first_form = []
    for jr in range(4):
        mine = jnp.where(lane // 32 == jr, whole, 0.0)
        mine = mine + pltpu.roll(mine, 64, 1)
        mine = mine + pltpu.roll(mine, 32, 1)
        first_form.append(stacked(mine))
    first_form = jnp.concatenate(first_form, 0)
    second_form = jnp.concatenate(
        [stacked(jnp.concatenate([q] * 4, 0).T) for q in quarters], 0
    )

    spots_in.wait()
    for j in range(PAIRS):
        left = rows_ref[mode_rows(0, j), :]
        right = rows_ref[mode_rows(1, j), :]
        lr, li, rr, ri = left[:8], left[8:], right[:8], right[8:]
        w_ref[j * 16 : j * 16 + 8, :] = lr * rr - li * ri
        w_ref[j * 16 + 8 : j * 16 + 16, :] = lr * ri + li * rr

    def operand(re, im):
        head, rest = heads(jnp.concatenate([re, im], 1))
        return jnp.concatenate([head, rest, head, rest], 0)

    for s in range(8):
        ur, ui = modes_at(0, 0, s), modes_at(0, 1, s)
        coupled = dot(first_form, operand(ur, ui))
        total_re = total_im = 0.0
        for j in range(PAIRS):
            row = ((j % 4) * 4 + j // 4) * 32
            cr, ci = coupled[row : row + 32, :128], coupled[row : row + 32, 128:]
            wr = w_ref[j * 16 + s : j * 16 + s + 1, :]
            wi = w_ref[j * 16 + 8 + s : j * 16 + 9 + s, :]
            total_re += cr * wr + ci * wi
            total_im += cr * wi - ci * wr
        gr = 2.0 * (ur - kerr_scale * total_im - modes_at(32, 0, s))
        gi = 2.0 * (ui + kerr_scale * total_re - modes_at(32, 1, s))
        spread = dot(second_form, operand(kerr_scale * gi, -kerr_scale * gr))
        for j in range(PAIRS):
            sr, si = spread[j * 32 : j * 32 + 32, :128], spread[j * 32 : j * 32 + 32, 128:]
            wr = w_ref[j * 16 + s : j * 16 + s + 1, :]
            wi = w_ref[j * 16 + 8 + s : j * 16 + 9 + s, :]
            gr += sr * wr + si * wi
            gi += sr * wi - si * wr
            gw_ref[j * 16 + s : j * 16 + s + 1, :] = jnp.sum(
                sr * ur - si * ui, axis=0, keepdims=True
            )
            gw_ref[j * 16 + 8 + s : j * 16 + 9 + s, :] = jnp.sum(
                sr * ui + si * ur, axis=0, keepdims=True
            )
        for m in range(2):
            for part, g in enumerate((gr, gi)):
                out_ref[pl.ds(m * 16 + part * 8 + s, OWNERS, stride=32), :] = g[
                    m * 16 : m * 16 + 16
                ]

    for j in range(PAIRS):
        gwr, gwi = gw_ref[j * 16 : j * 16 + 8, :], gw_ref[j * 16 + 8 : j * 16 + 16, :]
        for here, other, sum_ref in ((0, 1, out_ref), (1, 0, other_ref)):
            factor = rows_ref[mode_rows(other, j), :]
            fr, fi = factor[:8], factor[8:]
            spot = mode_rows(2 + here, j)
            sum_ref[spot, :] = sum_ref[spot, :] + jnp.concatenate(
                [gwr * fr + gwi * fi, gwi * fr - gwr * fi], 0
            )
    out_ref[...] = out_ref[...] + other_ref[...]


VMEM, HBM = (pl.BlockSpec(memory_space=space) for space in (pltpu.VMEM, pltpu.HBM))


def in_hbm(x):
    return pltpu.with_memory_space_constraint(x, pltpu.HBM)


def call(kernel, shapes, *args, scratch=(), specs=None, out=pltpu.VMEM):
    shapes = [out(shape, f32) if type(shape) is tuple else shape for shape in shapes]
    results = pl.pallas_call(
        kernel,
        out_shape=shapes,
        in_specs=specs or [VMEM] * len(args),
        out_specs=[pl.BlockSpec(memory_space=out)] * len(shapes),
        scratch_shapes=list(scratch),
        compiler_params=pltpu.CompilerParams(vmem_limit_bytes=24 * 1024 * 1024),
    )(*args)
    return results if len(shapes) > 1 else results[0]


def on_device(input_field, target_field, margin, pair_index, mode_beta, segment_kind):
    dft, twist = jnp.asarray(dft_parts()), jnp.asarray(twist_parts())
    both, phase, coupling, spots = call(
        gather_kernel,
        [(1024, 128), (2, 2, SIDE, SIDE), (8, 128), pltpu.VMEM((4, PAIRS), jnp.int32)],
        segment_kind,
        *map(
            in_hbm,
            (
                mode_beta.transpose(2, 1, 0),
                margin.transpose(0, 2, 1),
                pair_index.T,
                input_field,
                target_field,
            ),
        ),
        scratch=[
            pltpu.VMEM((2, PAIRS), jnp.int32),
            pltpu.VMEM((3, 2, mode_beta.shape[0]), f32),
            pltpu.VMEM((2, PAIRS, MODES), f32),
            pltpu.VMEM((2, 8, 2, 2, 2048), f32),
            pltpu.SemaphoreType.DMA((3,)),
            pltpu.SemaphoreType.DMA((2, 8)),
        ],
        specs=[pl.BlockSpec(memory_space=pltpu.SMEM)] + [HBM] * 5,
    )
    both = lax.all_to_all(both.reshape(8, 128, 128), "tm", 0, 0, tiled=True).reshape(1024, 128)
    packed = call(forward_kernel, [(OWNERS * BLOCK, 128)], both, coupling, dft, twist, phase)
    packed = lax.all_to_all(packed.reshape(OWNERS, BLOCK, 128), "mode", 0, 0, tiled=True)
    cotangent = call(
        kerr_kernel,
        [(512, 128)],
        spots,
        packed.reshape(OWNERS * BLOCK, 128),
        scratch=[
            pltpu.SMEM((4, PAIRS), jnp.int32),
            pltpu.VMEM((256, 128), f32),
            pltpu.VMEM((256, 128), f32),
            pltpu.VMEM((512, 128), f32),
            pltpu.SemaphoreType.DMA,
        ],
        specs=[VMEM, VMEM],
    )
    cotangent = lax.all_to_all(cotangent.reshape(OWNERS, 32, 128), "mode", 0, 0, tiled=True)
    gradient = call(
        backward_kernel, [(512, 128)], cotangent.reshape(512, 128), dft, twist, phase
    )
    gradient = lax.all_to_all(gradient.reshape(8, 64, 128), "tm", 0, 0, tiled=True)
    return call(
        scatter_kernel,
        [(2, 8, 2, 2048)],
        gradient.reshape(512, 128),
        scratch=[pltpu.VMEM((8, 2, 2, 2048), f32), pltpu.SemaphoreType.DMA((8,))],
        out=pltpu.HBM,
    )


def solution(mesh):
    field = P(None, "dp", "mode", "tm")
    return jax.shard_map(
        on_device,
        mesh=mesh,
        in_specs=(field, field, P("mode", None, None), P(), P(None, "mode", None), P()),
        out_specs=field,
        check_vma=False,
    )
```

```python
import jax
import jax.numpy as jnp
import numpy as np
from jax import lax
from jax.experimental import pallas as pl
from jax.experimental.pallas import tpu as pltpu
from jax.sharding import PartitionSpec as P

f32, bf16 = jnp.float32, jnp.bfloat16
kerr_scale = 0.1
SIDE = 128
TOTAL = SIDE * SIDE
MODES, PAIRS = 32, 16
OWNERS = 16
TIMES = 8
BLOCK = 72


def dft_parts():
    a = np.arange(SIDE)
    angle = 2.0 * np.pi * (np.outer(a, a) % SIDE) / SIDE
    parts = []
    for table in (np.cos(angle), np.sin(angle)):
        head = table.astype(np.float32).astype(bf16)
        parts += [head, (table - head.astype(np.float64)).astype(np.float32).astype(bf16)]
    return np.stack(parts)


def twist_parts():
    a = np.arange(SIDE)
    angle = 2.0 * np.pi * np.outer(a, a) / TOTAL
    return np.stack([np.cos(angle), np.sin(angle)]).astype(np.float32)


def heads(x):
    head = x.astype(bf16)
    return head, (x - head.astype(f32)).astype(bf16)


def dot(a, b):
    return jnp.dot(a, b, preferred_element_type=f32)


def real_form(cos, sin):
    return jnp.concatenate(
        [jnp.concatenate([cos, sin], 1), jnp.concatenate([-sin, cos], 1)], 0
    )


def disperse_modes(series, dft, twist, phase, sign):
    ch, cl, sh, sl = (dft[q] for q in range(4))
    plus = (real_form(ch, sh), real_form(cl, sl))
    minus = (real_form(ch, -sh), real_form(cl, -sl))

    def left(form, x):
        head, rest = heads(x)
        return dot(
            jnp.concatenate([form[0], form[0], form[1]], 1),
            jnp.concatenate([head, rest, head], 0),
        )

    def right(form, x):
        head, rest = heads(x)
        return dot(
            jnp.concatenate([head, rest, head], 1),
            jnp.concatenate([form[0], form[0], form[1]], 0),
        )

    def beside(parts):
        return jnp.concatenate(parts, 1)

    def below(parts):
        return jnp.concatenate(parts, 0)

    def quadrants(x):
        return (x[:SIDE, :SIDE], x[SIDE:, :SIDE]), (x[:SIDE, SIDE:], x[SIDE:, SIDE:])

    tc, ts = twist[0], twist[1]
    twisted = []
    for m, (yr, yi) in enumerate(quadrants(left(plus, beside([below(pair) for pair in series])))):
        pc, ps = phase[0, m], sign * phase[1, m]
        z = right(minus, beside([yr * tc + yi * ts, yi * tc - yr * ts]))
        zr, zi = z[:, :SIDE], z[:, SIDE:]
        y = right(plus, beside([zr * pc - zi * ps, zr * ps + zi * pc]))
        yr, yi = y[:, :SIDE], y[:, SIDE:]
        twisted.append(below([yr * tc - yi * ts, yr * ts + yi * tc]))
    return quadrants(left(minus, beside(twisted)))


def cos_sin(angle):
    turn = jnp.floor(angle * (2.0 / np.pi) + 0.5)
    x = angle - turn * 1.5703125
    x = x - turn * 4.837512969970703e-4
    x = x - turn * 7.549789954891882e-8
    z = x * x
    sine = x + x * z * (-1.6666654611e-1 + z * (8.3321608736e-3 - z * 1.9515295891e-4))
    cosine = 1.0 - 0.5 * z + z * z * (
        4.166664568298827e-2 + z * (-1.388731625493765e-3 + z * 2.443315711809948e-5)
    )
    quarter = turn.astype(jnp.int32)
    odd = quarter & 1 == 1
    first, second = jnp.where(odd, sine, cosine), jnp.where(odd, cosine, sine)
    return (
        jnp.where((quarter + 1) & 2 == 2, -first, first),
        jnp.where(quarter & 2 == 2, -second, second),
    )


def gather_kernel(
    kind_ref, beta_hbm, margin_hbm, pair_hbm, field_ref, target_ref,
    out_ref, phase_ref, coupling_ref, spot_ref,
    pair_ref, beta_ref, margin_ref, held_ref, small_sems, sems,
):
    small = [
        pltpu.make_async_copy(there, here, small_sems.at[q])
        for q, (there, here) in enumerate(
            ((beta_hbm, beta_ref), (margin_hbm, margin_ref), (pair_hbm, pair_ref))
        )
    ]
    for copy in small:
        copy.start()
    order = [(b, what) for b in range(8) for what in range(2)]
    copies = {}
    for b, what in order:
        copies[b, what] = pltpu.make_async_copy(
            (field_ref, target_ref)[what].at[:, b], held_ref.at[what, b], sems.at[what, b]
        )
        copies[b, what].start()

    for b, what in order:
        copies[b, what].wait()
        for part in range(2):
            spot = b * 128 + what * 64 + part * 32
            for k in range(16):
                out_ref[pl.ds(spot + k, 2, stride=16), :] = held_ref[
                    what, b, part, :, k * 128 : k * 128 + 128
                ]
    for copy in small:
        copy.wait()
    pair = pair_ref[...]
    for q, block in enumerate((BLOCK, 32)):
        spot_ref[2 * q : 2 * q + 2, :] = (pair >> 1) * block + (pair & 1) * 16
    lane = lax.broadcasted_iota(jnp.int32, (128, 128), 1)
    source = lax.broadcasted_iota(jnp.int32, (128, 128), 0)
    place = source // 32 * 32 + source % 2 * 16 + source % 32 // 2
    wide = jnp.zeros((16, 96), f32)
    flat = []
    for p in range(2):
        rows = jnp.concatenate([margin_ref[p], wide], 1)
        flat.append(
            sum(
                pltpu.roll(
                    jnp.concatenate([rows[4 * q + jr : 4 * q + jr + 1] for q in range(4)], 0),
                    32 * jr,
                    1,
                )
                if jr
                else jnp.concatenate([rows[4 * q : 4 * q + 1] for q in range(4)], 0)
                for jr in range(4)
            )
        )
    coupling_ref[...] = jnp.dot(
        jnp.concatenate(flat, 0),
        (place == lane).astype(f32),
        precision=lax.Precision.HIGHEST,
        preferred_element_type=f32,
    )

    kinds = lax.broadcasted_iota(jnp.int32, beta_ref.shape, 2)
    table = jnp.sum(jnp.where(kinds == kind_ref[0], beta_ref[...], 0.0), axis=2, keepdims=True)
    index = source + SIDE * lane
    signed = jnp.where(index < TOTAL // 2, index, index - TOTAL).astype(f32)
    omega = signed * (8.0 / TOTAL)
    for m in range(2):
        first, second, third = (table[q, m : m + 1] for q in range(3))
        phase = first * omega + second * omega**2 / 2.0 + third * omega**3 / 6.0
        cosine, sine = cos_sin(phase)
        phase_ref[0, m] = cosine * (1.0 / TOTAL)
        phase_ref[1, m] = sine * (1.0 / TOTAL)


def scatter_kernel(rows_ref, out_ref, held_ref, sems):
    copies = []
    for b in range(8):
        for part in range(2):
            for k in range(16):
                held_ref[b, part, :, k * 128 : k * 128 + 128] = rows_ref[
                    pl.ds(b * 64 + part * 32 + k, 2, stride=16), :
                ]
        copies.append(pltpu.make_async_copy(held_ref.at[b], out_ref.at[:, b], sems.at[b]))
        copies[-1].start()
    for copy in copies:
        copy.wait()


def forward_kernel(rows_ref, margin_ref, dft_ref, twist_ref, phase_ref, out_ref):
    def chunk(s, what, m, part):
        spot = s * 128 + what * 64 + part * 32 + m * 16
        return rows_ref[spot : spot + 16, :]

    fields = [
        tuple(
            jnp.concatenate([chunk(s, 0, m, part) for s in range(TIMES)], 0) for part in range(2)
        )
        for m in range(2)
    ]
    for m in range(2):
        for part in range(2):
            for s in range(TIMES):
                rows = chunk(s, 1, m, part)
                for h in range(2):
                    spot = (2 * s + h) * BLOCK + 32 + m * 16 + part * 8
                    out_ref[spot : spot + 8, :] = rows[8 * h : 8 * h + 8]
    margin = margin_ref[...]
    for k in range(OWNERS):
        out_ref[k * BLOCK + 64 : k * BLOCK + 72, :] = margin
    result = disperse_modes(fields, dft_ref, twist_ref, phase_ref, 1.0)
    for m in range(2):
        for part in range(2):
            for k in range(OWNERS):
                spot = k * BLOCK + m * 16 + part * 8
                out_ref[spot : spot + 8, :] = result[m][part][8 * k : 8 * k + 8]


def backward_kernel(rows_ref, dft_ref, twist_ref, phase_ref, out_ref):
    fields = [
        tuple(
            jnp.concatenate(
                [
                    rows_ref[k * 32 + m * 16 + part * 8 : k * 32 + m * 16 + part * 8 + 8, :]
                    for k in range(OWNERS)
                ],
                0,
            )
            for part in range(2)
        )
        for m in range(2)
    ]
    result = disperse_modes(fields, dft_ref, twist_ref, phase_ref, -1.0)
    for m in range(2):
        for part in range(2):
            for s in range(TIMES):
                spot = s * 64 + part * 32 + m * 16
                out_ref[spot : spot + 16, :] = result[m][part][16 * s : 16 * s + 16]


def kerr_kernel(spot_vmem, rows_ref, out_ref, spot_ref, w_ref, gw_ref, other_ref, sem):
    spots_in = pltpu.make_async_copy(spot_vmem, spot_ref, sem)
    spots_in.start()

    def by_owner(row):
        return rows_ref[pl.ds(row, OWNERS, stride=BLOCK), :]

    def modes_at(first, part, s):
        return jnp.concatenate(
            [by_owner(first + m * 16 + part * 8 + s) for m in range(2)], 0
        )

    def mode_rows(kind, j):
        return pl.ds(pl.multiple_of(spot_ref[kind, j], 8), 16)

    other_ref[...] = jnp.zeros_like(other_ref)
    lane = lax.broadcasted_iota(jnp.int32, (128, 128), 1)

    def stacked(x):
        head = x.astype(bf16).astype(f32)
        return jnp.where(lane < 64, head, x - head).astype(bf16)

    quarters = [
        jnp.concatenate([by_owner(64 + m * 4 + q) for m in range(2)], 0) for q in range(4)
    ]
    whole = jnp.concatenate(quarters, 0)
    first_form = []
    for jr in range(4):
        mine = jnp.where(lane // 32 == jr, whole, 0.0)
        mine = mine + pltpu.roll(mine, 64, 1)
        mine = mine + pltpu.roll(mine, 32, 1)
        first_form.append(stacked(mine))
    first_form = jnp.concatenate(first_form, 0)
    second_form = jnp.concatenate(
        [stacked(jnp.concatenate([q] * 4, 0).T) for q in quarters], 0
    )

    spots_in.wait()
    for j in range(PAIRS):
        left = rows_ref[mode_rows(0, j), :]
        right = rows_ref[mode_rows(1, j), :]
        lr, li, rr, ri = left[:8], left[8:], right[:8], right[8:]
        w_ref[j * 16 : j * 16 + 8, :] = lr * rr - li * ri
        w_ref[j * 16 + 8 : j * 16 + 16, :] = lr * ri + li * rr

    eighth = lax.broadcasted_iota(jnp.int32, (8, 128), 0)

    def over_vectors(x):
        return x[:8] + x[8:16] + (x[16:24] + x[24:])

    def merged(a, b, step):
        mine = eighth & step == 0
        return jnp.where(mine, a, b) + pltpu.roll(jnp.where(mine, b, a), step, 0)

    def operand(re, im):
        head, rest = heads(jnp.concatenate([re, im], 1))
        return jnp.concatenate([head, rest, head, rest], 0)

    for s in range(8):
        ur, ui = modes_at(0, 0, s), modes_at(0, 1, s)
        coupled = dot(first_form, operand(ur, ui))
        total_re = total_im = 0.0
        for j in range(PAIRS):
            row = ((j % 4) * 4 + j // 4) * 32
            cr, ci = coupled[row : row + 32, :128], coupled[row : row + 32, 128:]
            wr = w_ref[j * 16 + s : j * 16 + s + 1, :]
            wi = w_ref[j * 16 + 8 + s : j * 16 + 9 + s, :]
            total_re += cr * wr + ci * wi
            total_im += cr * wi - ci * wr
        gr = 2.0 * (ur - kerr_scale * total_im - modes_at(32, 0, s))
        gi = 2.0 * (ui + kerr_scale * total_re - modes_at(32, 1, s))
        sums = []
        spread = dot(second_form, operand(kerr_scale * gi, -kerr_scale * gr))
        for j in range(PAIRS):
            sr, si = spread[j * 32 : j * 32 + 32, :128], spread[j * 32 : j * 32 + 32, 128:]
            wr = w_ref[j * 16 + s : j * 16 + s + 1, :]
            wi = w_ref[j * 16 + 8 + s : j * 16 + 9 + s, :]
            gr += sr * wr + si * wi
            gi += sr * wi - si * wr
            sums += [over_vectors(sr * ur - si * ui), over_vectors(sr * ui + si * ur)]
            if len(sums) == 8:
                for step in (1, 2, 4):
                    sums = [merged(*two, step) for two in zip(sums[::2], sums[1::2])]
                gw_ref[pl.ds((j - 3) * 16 + s, 8, stride=8), :] = sums.pop()
        for m in range(2):
            for part, g in enumerate((gr, gi)):
                out_ref[pl.ds(m * 16 + part * 8 + s, OWNERS, stride=32), :] = g[
                    m * 16 : m * 16 + 16
                ]

    for j in range(PAIRS):
        gwr, gwi = gw_ref[j * 16 : j * 16 + 8, :], gw_ref[j * 16 + 8 : j * 16 + 16, :]
        for here, other, sum_ref in ((0, 1, out_ref), (1, 0, other_ref)):
            factor = rows_ref[mode_rows(other, j), :]
            fr, fi = factor[:8], factor[8:]
            spot = mode_rows(2 + here, j)
            sum_ref[spot, :] = sum_ref[spot, :] + jnp.concatenate(
                [gwr * fr + gwi * fi, gwi * fr - gwr * fi], 0
            )
    out_ref[...] = out_ref[...] + other_ref[...]


VMEM, HBM = (pl.BlockSpec(memory_space=space) for space in (pltpu.VMEM, pltpu.HBM))


def in_hbm(x):
    return pltpu.with_memory_space_constraint(x, pltpu.HBM)


def call(kernel, shapes, *args, scratch=(), specs=None, out=pltpu.VMEM):
    shapes = [out(shape, f32) if type(shape) is tuple else shape for shape in shapes]
    results = pl.pallas_call(
        kernel,
        out_shape=shapes,
        in_specs=specs or [VMEM] * len(args),
        out_specs=[pl.BlockSpec(memory_space=out)] * len(shapes),
        scratch_shapes=list(scratch),
        compiler_params=pltpu.CompilerParams(vmem_limit_bytes=24 * 1024 * 1024),
    )(*args)
    return results if len(shapes) > 1 else results[0]


def on_device(input_field, target_field, margin, pair_index, mode_beta, segment_kind):
    dft, twist = jnp.asarray(dft_parts()), jnp.asarray(twist_parts())
    both, phase, coupling, spots = call(
        gather_kernel,
        [(1024, 128), (2, 2, SIDE, SIDE), (8, 128), pltpu.VMEM((4, PAIRS), jnp.int32)],
        segment_kind,
        *map(
            in_hbm,
            (
                mode_beta.transpose(2, 1, 0),
                margin.transpose(0, 2, 1),
                pair_index.T,
                input_field,
                target_field,
            ),
        ),
        scratch=[
            pltpu.VMEM((2, PAIRS), jnp.int32),
            pltpu.VMEM((3, 2, mode_beta.shape[0]), f32),
            pltpu.VMEM((2, PAIRS, MODES), f32),
            pltpu.VMEM((2, 8, 2, 2, 2048), f32),
            pltpu.SemaphoreType.DMA((3,)),
            pltpu.SemaphoreType.DMA((2, 8)),
        ],
        specs=[pl.BlockSpec(memory_space=pltpu.SMEM)] + [HBM] * 5,
    )
    both = lax.all_to_all(both.reshape(8, 128, 128), "tm", 0, 0, tiled=True).reshape(1024, 128)
    packed = call(forward_kernel, [(OWNERS * BLOCK, 128)], both, coupling, dft, twist, phase)
    packed = lax.all_to_all(packed.reshape(OWNERS, BLOCK, 128), "mode", 0, 0, tiled=True)
    cotangent = call(
        kerr_kernel,
        [(512, 128)],
        spots,
        packed.reshape(OWNERS * BLOCK, 128),
        scratch=[
            pltpu.SMEM((4, PAIRS), jnp.int32),
            pltpu.VMEM((256, 128), f32),
            pltpu.VMEM((256, 128), f32),
            pltpu.VMEM((512, 128), f32),
            pltpu.SemaphoreType.DMA,
        ],
        specs=[VMEM, VMEM],
    )
    cotangent = lax.all_to_all(cotangent.reshape(OWNERS, 32, 128), "mode", 0, 0, tiled=True)
    gradient = call(
        backward_kernel, [(512, 128)], cotangent.reshape(512, 128), dft, twist, phase
    )
    gradient = lax.all_to_all(gradient.reshape(8, 64, 128), "tm", 0, 0, tiled=True)
    return call(
        scatter_kernel,
        [(2, 8, 2, 2048)],
        gradient.reshape(512, 128),
        scratch=[pltpu.VMEM((8, 2, 2, 2048), f32), pltpu.SemaphoreType.DMA((8,))],
        out=pltpu.HBM,
    )


def solution(mesh):
    field = P(None, "dp", "mode", "tm")
    return jax.shard_map(
        on_device,
        mesh=mesh,
        in_specs=(field, field, P("mode", None, None), P(), P(None, "mode", None), P()),
        out_specs=field,
        check_vma=False,
    )
```

```python
import jax
import jax.numpy as jnp
import numpy as np
from jax import lax
from jax.experimental import pallas as pl
from jax.experimental.pallas import tpu as pltpu
from jax.sharding import PartitionSpec as P

f32, bf16 = jnp.float32, jnp.bfloat16
kerr_scale = 0.1
SIDE = 128
TOTAL = SIDE * SIDE
MODES, PAIRS = 32, 16
OWNERS = 16
TIMES = 8
BLOCK = 72


def dft_parts():
    a = np.arange(SIDE)
    angle = 2.0 * np.pi * (np.outer(a, a) % SIDE) / SIDE
    parts = []
    for table in (np.cos(angle), np.sin(angle)):
        head = table.astype(np.float32).astype(bf16)
        parts += [head, (table - head.astype(np.float64)).astype(np.float32).astype(bf16)]
    return np.stack(parts)


def twist_parts():
    a = np.arange(SIDE)
    angle = 2.0 * np.pi * np.outer(a, a) / TOTAL
    return np.stack([np.cos(angle), np.sin(angle)]).astype(np.float32)


def heads(x):
    head = x.astype(bf16)
    return head, (x - head.astype(f32)).astype(bf16)


def dot(a, b):
    return jnp.dot(a, b, preferred_element_type=f32)


def real_form(cos, sin):
    return jnp.concatenate(
        [jnp.concatenate([cos, sin], 1), jnp.concatenate([-sin, cos], 1)], 0
    )


def disperse_modes(series, dft, twist, phase, sign):
    ch, cl, sh, sl = (dft[q] for q in range(4))
    plus = (real_form(ch, sh), real_form(cl, sl))
    minus = (real_form(ch, -sh), real_form(cl, -sl))

    def left(form, x):
        head, rest = heads(x)
        return dot(
            jnp.concatenate([form[0], form[0], form[1]], 1),
            jnp.concatenate([head, rest, head], 0),
        )

    def right(form, x):
        head, rest = heads(x)
        return dot(
            jnp.concatenate([head, rest, head], 1),
            jnp.concatenate([form[0], form[0], form[1]], 0),
        )

    def beside(parts):
        return jnp.concatenate(parts, 1)

    def below(parts):
        return jnp.concatenate(parts, 0)

    def quadrants(x):
        return (x[:SIDE, :SIDE], x[SIDE:, :SIDE]), (x[:SIDE, SIDE:], x[SIDE:, SIDE:])

    tc, ts = twist[0], twist[1]
    twisted = []
    for m, (yr, yi) in enumerate(quadrants(left(plus, beside([below(pair) for pair in series])))):
        pc, ps = phase[0, m], sign * phase[1, m]
        z = right(minus, beside([yr * tc + yi * ts, yi * tc - yr * ts]))
        zr, zi = z[:, :SIDE], z[:, SIDE:]
        y = right(plus, beside([zr * pc - zi * ps, zr * ps + zi * pc]))
        yr, yi = y[:, :SIDE], y[:, SIDE:]
        twisted.append(below([yr * tc - yi * ts, yr * ts + yi * tc]))
    return quadrants(left(minus, beside(twisted)))


def cos_sin(angle):
    turn = jnp.floor(angle * (2.0 / np.pi) + 0.5)
    x = angle - turn * 1.5703125
    x = x - turn * 4.837512969970703e-4
    x = x - turn * 7.549789954891882e-8
    z = x * x
    sine = x + x * z * (-1.6666654611e-1 + z * (8.3321608736e-3 - z * 1.9515295891e-4))
    cosine = 1.0 - 0.5 * z + z * z * (
        4.166664568298827e-2 + z * (-1.388731625493765e-3 + z * 2.443315711809948e-5)
    )
    quarter = turn.astype(jnp.int32)
    odd = quarter & 1 == 1
    first, second = jnp.where(odd, sine, cosine), jnp.where(odd, cosine, sine)
    return (
        jnp.where((quarter + 1) & 2 == 2, -first, first),
        jnp.where(quarter & 2 == 2, -second, second),
    )


def gather_kernel(
    kind_ref, beta_hbm, margin_hbm, pair_hbm, field_ref, target_ref,
    out_ref, phase_ref, coupling_ref, spot_ref,
    pair_ref, beta_ref, margin_ref, held_ref, small_sems, sems,
):
    small = [
        pltpu.make_async_copy(there, here, small_sems.at[q])
        for q, (there, here) in enumerate(
            ((beta_hbm, beta_ref), (margin_hbm, margin_ref), (pair_hbm, pair_ref))
        )
    ]
    for copy in small:
        copy.start()
    order = [(b, what) for b in range(8) for what in range(2)]
    copies = {}
    for b, what in order:
        copies[b, what] = pltpu.make_async_copy(
            (field_ref, target_ref)[what].at[:, b], held_ref.at[what, b], sems.at[what, b]
        )
        copies[b, what].start()

    for b, what in order:
        copies[b, what].wait()
        for part in range(2):
            spot = b * 128 + what * 64 + part * 32
            for k in range(16):
                out_ref[pl.ds(spot + k, 2, stride=16), :] = held_ref[
                    what, b, part, :, k * 128 : k * 128 + 128
                ]
    for copy in small:
        copy.wait()
    pair = pair_ref[...]
    for q, block in enumerate((BLOCK, 32)):
        spot_ref[2 * q : 2 * q + 2, :] = (pair >> 1) * block + (pair & 1) * 16
    lane = lax.broadcasted_iota(jnp.int32, (128, 128), 1)
    source = lax.broadcasted_iota(jnp.int32, (128, 128), 0)
    place = source // 32 * 32 + source % 2 * 16 + source % 32 // 2
    wide = jnp.zeros((16, 96), f32)
    flat = []
    for p in range(2):
        rows = jnp.concatenate([margin_ref[p], wide], 1)
        flat.append(
            sum(
                pltpu.roll(
                    jnp.concatenate([rows[4 * q + jr : 4 * q + jr + 1] for q in range(4)], 0),
                    32 * jr,
                    1,
                )
                if jr
                else jnp.concatenate([rows[4 * q : 4 * q + 1] for q in range(4)], 0)
                for jr in range(4)
            )
        )
    coupling_ref[...] = jnp.dot(
        jnp.concatenate(flat, 0),
        (place == lane).astype(f32),
        precision=lax.Precision.HIGHEST,
        preferred_element_type=f32,
    )

    kinds = lax.broadcasted_iota(jnp.int32, beta_ref.shape, 2)
    table = jnp.sum(jnp.where(kinds == kind_ref[0], beta_ref[...], 0.0), axis=2, keepdims=True)
    index = source + SIDE * lane
    signed = jnp.where(index < TOTAL // 2, index, index - TOTAL).astype(f32)
    omega = signed * (8.0 / TOTAL)
    for m in range(2):
        first, second, third = (table[q, m : m + 1] for q in range(3))
        phase = first * omega + second * omega**2 / 2.0 + third * omega**3 / 6.0
        cosine, sine = cos_sin(phase)
        phase_ref[0, m] = cosine * (1.0 / TOTAL)
        phase_ref[1, m] = sine * (1.0 / TOTAL)


def scatter_kernel(rows_ref, out_ref, held_ref, sems):
    copies = []
    for b in range(8):
        for part in range(2):
            for k in range(16):
                held_ref[b, part, :, k * 128 : k * 128 + 128] = rows_ref[
                    pl.ds(b * 64 + part * 32 + k, 2, stride=16), :
                ]
        copies.append(pltpu.make_async_copy(held_ref.at[b], out_ref.at[:, b], sems.at[b]))
        copies[-1].start()
    for copy in copies:
        copy.wait()


def forward_kernel(rows_ref, margin_ref, dft_ref, twist_ref, phase_ref, out_ref):
    def chunk(s, what, m, part):
        spot = s * 128 + what * 64 + part * 32 + m * 16
        return rows_ref[spot : spot + 16, :]

    fields = [
        tuple(
            jnp.concatenate([chunk(s, 0, m, part) for s in range(TIMES)], 0) for part in range(2)
        )
        for m in range(2)
    ]
    for m in range(2):
        for part in range(2):
            for s in range(TIMES):
                rows = chunk(s, 1, m, part)
                for h in range(2):
                    spot = (2 * s + h) * BLOCK + 32 + m * 16 + part * 8
                    out_ref[spot : spot + 8, :] = rows[8 * h : 8 * h + 8]
    margin = margin_ref[...]
    for k in range(OWNERS):
        out_ref[k * BLOCK + 64 : k * BLOCK + 72, :] = margin
    result = disperse_modes(fields, dft_ref, twist_ref, phase_ref, 1.0)
    for m in range(2):
        for part in range(2):
            for k in range(OWNERS):
                spot = k * BLOCK + m * 16 + part * 8
                out_ref[spot : spot + 8, :] = result[m][part][8 * k : 8 * k + 8]


def backward_kernel(rows_ref, dft_ref, twist_ref, phase_ref, out_ref):
    fields = [
        tuple(
            jnp.concatenate(
                [
                    rows_ref[k * 32 + m * 16 + part * 8 : k * 32 + m * 16 + part * 8 + 8, :]
                    for k in range(OWNERS)
                ],
                0,
            )
            for part in range(2)
        )
        for m in range(2)
    ]
    result = disperse_modes(fields, dft_ref, twist_ref, phase_ref, -1.0)
    for m in range(2):
        for part in range(2):
            for s in range(TIMES):
                spot = s * 64 + part * 32 + m * 16
                out_ref[spot : spot + 16, :] = result[m][part][16 * s : 16 * s + 16]


def kerr_kernel(spot_vmem, rows_ref, out_ref, spot_ref, w_ref, gw_ref, other_ref, sem):
    spots_in = pltpu.make_async_copy(spot_vmem, spot_ref, sem)
    spots_in.start()

    def by_owner(row):
        return rows_ref[pl.ds(row, OWNERS, stride=BLOCK), :]

    def modes_at(first, part, s):
        return jnp.concatenate(
            [by_owner(first + m * 16 + part * 8 + s) for m in range(2)], 0
        )

    def mode_rows(kind, j):
        return pl.ds(pl.multiple_of(spot_ref[kind, j], 8), 16)

    other_ref[...] = jnp.zeros_like(other_ref)
    lane = lax.broadcasted_iota(jnp.int32, (128, 128), 1)

    def stacked(x):
        head = x.astype(bf16).astype(f32)
        return jnp.where(lane < 64, head, x - head).astype(bf16)

    quarters = [
        jnp.concatenate([by_owner(64 + m * 4 + q) for m in range(2)], 0) for q in range(4)
    ]
    whole = jnp.concatenate(quarters, 0)
    first_form = []
    for jr in range(4):
        mine = jnp.where(lane // 32 == jr, whole, 0.0)
        mine = mine + pltpu.roll(mine, 64, 1)
        mine = mine + pltpu.roll(mine, 32, 1)
        first_form.append(stacked(mine))
    first_form = jnp.concatenate(first_form, 0)
    second_form = jnp.concatenate(
        [stacked(jnp.concatenate([q] * 4, 0).T) for q in quarters], 0
    )

    spots_in.wait()
    for j in range(PAIRS):
        left = rows_ref[mode_rows(0, j), :]
        right = rows_ref[mode_rows(1, j), :]
        lr, li, rr, ri = left[:8], left[8:], right[:8], right[8:]
        w_ref[j * 16 : j * 16 + 8, :] = lr * rr - li * ri
        w_ref[j * 16 + 8 : j * 16 + 16, :] = lr * ri + li * rr

    eighth = lax.broadcasted_iota(jnp.int32, (8, 128), 0)

    def over_vectors(x):
        return x[:8] + x[8:16] + (x[16:24] + x[24:])

    def merged(a, b, step):
        mine = eighth & step == 0
        return jnp.where(mine, a, b) + pltpu.roll(jnp.where(mine, b, a), step, 0)

    def operand(re, im):
        head, rest = heads(jnp.concatenate([re, im], 1))
        return jnp.concatenate([head, rest, head, rest], 0)

    def coupled_at(s):
        ur, ui = modes_at(0, 0, s), modes_at(0, 1, s)
        return ur, ui, dot(first_form, operand(ur, ui))

    later = coupled_at(0)
    for s in range(8):
        ur, ui, coupled = later
        total_re = total_im = 0.0
        for j in range(PAIRS):
            row = ((j % 4) * 4 + j // 4) * 32
            cr, ci = coupled[row : row + 32, :128], coupled[row : row + 32, 128:]
            wr = w_ref[j * 16 + s : j * 16 + s + 1, :]
            wi = w_ref[j * 16 + 8 + s : j * 16 + 9 + s, :]
            total_re += cr * wr + ci * wi
            total_im += cr * wi - ci * wr
        gr = 2.0 * (ur - kerr_scale * total_im - modes_at(32, 0, s))
        gi = 2.0 * (ui + kerr_scale * total_re - modes_at(32, 1, s))
        sums = []
        spread = dot(second_form, operand(kerr_scale * gi, -kerr_scale * gr))
        if s < 7:
            later = coupled_at(s + 1)
        for j in range(PAIRS):
            sr, si = spread[j * 32 : j * 32 + 32, :128], spread[j * 32 : j * 32 + 32, 128:]
            wr = w_ref[j * 16 + s : j * 16 + s + 1, :]
            wi = w_ref[j * 16 + 8 + s : j * 16 + 9 + s, :]
            gr += sr * wr + si * wi
            gi += sr * wi - si * wr
            sums += [over_vectors(sr * ur - si * ui), over_vectors(sr * ui + si * ur)]
            if len(sums) == 8:
                for step in (1, 2, 4):
                    sums = [merged(*two, step) for two in zip(sums[::2], sums[1::2])]
                gw_ref[pl.ds((j - 3) * 16 + s, 8, stride=8), :] = sums.pop()
        for m in range(2):
            for part, g in enumerate((gr, gi)):
                out_ref[pl.ds(m * 16 + part * 8 + s, OWNERS, stride=32), :] = g[
                    m * 16 : m * 16 + 16
                ]

    for j in range(PAIRS):
        gwr, gwi = gw_ref[j * 16 : j * 16 + 8, :], gw_ref[j * 16 + 8 : j * 16 + 16, :]
        for here, other, sum_ref in ((0, 1, out_ref), (1, 0, other_ref)):
            factor = rows_ref[mode_rows(other, j), :]
            fr, fi = factor[:8], factor[8:]
            spot = mode_rows(2 + here, j)
            sum_ref[spot, :] = sum_ref[spot, :] + jnp.concatenate(
                [gwr * fr + gwi * fi, gwi * fr - gwr * fi], 0
            )
    out_ref[...] = out_ref[...] + other_ref[...]


VMEM, HBM = (pl.BlockSpec(memory_space=space) for space in (pltpu.VMEM, pltpu.HBM))


def in_hbm(x):
    return pltpu.with_memory_space_constraint(x, pltpu.HBM)


def call(kernel, shapes, *args, scratch=(), specs=None, out=pltpu.VMEM):
    shapes = [out(shape, f32) if type(shape) is tuple else shape for shape in shapes]
    results = pl.pallas_call(
        kernel,
        out_shape=shapes,
        in_specs=specs or [VMEM] * len(args),
        out_specs=[pl.BlockSpec(memory_space=out)] * len(shapes),
        scratch_shapes=list(scratch),
        compiler_params=pltpu.CompilerParams(vmem_limit_bytes=24 * 1024 * 1024),
    )(*args)
    return results if len(shapes) > 1 else results[0]


def on_device(input_field, target_field, margin, pair_index, mode_beta, segment_kind):
    dft, twist = jnp.asarray(dft_parts()), jnp.asarray(twist_parts())
    both, phase, coupling, spots = call(
        gather_kernel,
        [(1024, 128), (2, 2, SIDE, SIDE), (8, 128), pltpu.VMEM((4, PAIRS), jnp.int32)],
        segment_kind,
        *map(
            in_hbm,
            (
                mode_beta.transpose(2, 1, 0),
                margin.transpose(0, 2, 1),
                pair_index.T,
                input_field,
                target_field,
            ),
        ),
        scratch=[
            pltpu.VMEM((2, PAIRS), jnp.int32),
            pltpu.VMEM((3, 2, mode_beta.shape[0]), f32),
            pltpu.VMEM((2, PAIRS, MODES), f32),
            pltpu.VMEM((2, 8, 2, 2, 2048), f32),
            pltpu.SemaphoreType.DMA((3,)),
            pltpu.SemaphoreType.DMA((2, 8)),
        ],
        specs=[pl.BlockSpec(memory_space=pltpu.SMEM)] + [HBM] * 5,
    )
    both = lax.all_to_all(both.reshape(8, 128, 128), "tm", 0, 0, tiled=True).reshape(1024, 128)
    packed = call(forward_kernel, [(OWNERS * BLOCK, 128)], both, coupling, dft, twist, phase)
    packed = lax.all_to_all(packed.reshape(OWNERS, BLOCK, 128), "mode", 0, 0, tiled=True)
    cotangent = call(
        kerr_kernel,
        [(512, 128)],
        spots,
        packed.reshape(OWNERS * BLOCK, 128),
        scratch=[
            pltpu.SMEM((4, PAIRS), jnp.int32),
            pltpu.VMEM((256, 128), f32),
            pltpu.VMEM((256, 128), f32),
            pltpu.VMEM((512, 128), f32),
            pltpu.SemaphoreType.DMA,
        ],
        specs=[VMEM, VMEM],
    )
    cotangent = lax.all_to_all(cotangent.reshape(OWNERS, 32, 128), "mode", 0, 0, tiled=True)
    gradient = call(
        backward_kernel, [(512, 128)], cotangent.reshape(512, 128), dft, twist, phase
    )
    gradient = lax.all_to_all(gradient.reshape(8, 64, 128), "tm", 0, 0, tiled=True)
    return call(
        scatter_kernel,
        [(2, 8, 2, 2048)],
        gradient.reshape(512, 128),
        scratch=[pltpu.VMEM((8, 2, 2, 2048), f32), pltpu.SemaphoreType.DMA((8,))],
        out=pltpu.HBM,
    )


def solution(mesh):
    field = P(None, "dp", "mode", "tm")
    return jax.shard_map(
        on_device,
        mesh=mesh,
        in_specs=(field, field, P("mode", None, None), P(), P(None, "mode", None), P()),
        out_specs=field,
        check_vma=False,
    )
```
